512 devices in a mesh: space: 64 (over x, y, z_hi), filt: 8 (over z_lo, core).
Axes of the slice: x: 4, y: 8, z: 8 (z_hi: 2, z_lo: 4; z = z_hi * 4 + z_lo), core: 2. Of those that a mesh axis runs over, the one named last changes fastest.
Arguments:
- volume: bfloat16 [64, 8, 32, 384], P('space', None, None, 'filt'), may hold values from -6 to 6
- kernel: bfloat16 [3, 3, 3, 384, 384], P(None, None, None, 'filt'), may hold values from -0.0625 to 0.0625
- cotangent: bfloat16 [64, 8, 32, 384], P('space', None, None, 'filt'), may hold values from -6 to 6
Outputs:
- response: bfloat16 [64, 8, 32, 384], P('space', None, None, 'filt')
- volume_grad: bfloat16 [64, 8, 32, 384], P('space', None, None, 'filt')
- kernel_grad: float32 [3, 3, 3, 384, 384], P(None, None, None, 'filt')
The draws below stay inside these ranges and needn't reach their ends.
All inputs are finite; a program needn't handle non-finite values.
Results may differ from the reference program's by a relative error of at most 0.001.
Values may be sent and summed in bfloat16 or wider, within the bound.
No kernel may reach another device: no remote copies, remote signals or barrier semaphores. Data moves between devices by JAX's collectives and lax.ppermute only.
A program may use at most 64 MiB of HBM per device.

```python
import jax
import jax.numpy as jnp
from jax import lax

CHANNELS = 384
HEIGHT = 8
WIDTH = 32
DEPTH = 64


def levels(own_key, dims, pieces, smallest, largest):
    def one(axis_at, blocks):
        draws = jax.random.uniform(jax.random.fold_in(jax.random.fold_in(own_key, 6), axis_at), (blocks,), jnp.float32, smallest / len(pieces), largest / len(pieces))
        return jnp.repeat(jnp.exp(draws), dims[axis_at] // blocks).reshape((-1,) + (1,) * (len(dims) - axis_at - 1))

    level = one(*pieces[0])
    for cut in pieces[1:]:
        level = level * one(*cut)
    return level


def normal_values(own_key, dims, spread, bound, shards=(), dtype=jnp.bfloat16):
    array = jax.random.normal(own_key, dims, jnp.float32) * spread
    if len(shards) > 0:
        array = levels(own_key, dims, shards, -0.22, 0.18) * array
    return jnp.clip(array, min=-bound, max=bound).astype(dtype)


def setup_inputs(seed: int = 0) -> dict:
    key_list = jax.random.split(jax.random.key(seed), 4)
    return {
        "volume": normal_values(key_list[0], (DEPTH, HEIGHT, WIDTH, CHANNELS), 1.0, 6.0, ((0, 64), (3, 8))),
        "kernel": normal_values(key_list[1], (3, 3, 3, CHANNELS, CHANNELS), (27 * CHANNELS) ** -0.5, 0.0625, ((3, 8),)),
        "cotangent": normal_values(key_list[2], (DEPTH, HEIGHT, WIDTH, CHANNELS), 1.0, 6.0, ((0, 64), (3, 8))),
    }


def reference(volume, kernel, cotangent):
    depth_total, grid_height, grid_width, channel_count = volume.shape
    rows_total = depth_total * grid_height * grid_width
    pad_spec = ((1, 1), (1, 1), (1, 1), (0, 0))
    padded = jnp.pad(volume, pad_spec)
    grad_padded = jnp.pad(cotangent, pad_spec)
    flat_grad = cotangent.reshape(rows_total, channel_count)
    response = jnp.zeros((rows_total, channel_count), jnp.float32)
    volume_grad = jnp.zeros((rows_total, channel_count), jnp.float32)
    grad_parts = []
    for depth_off in range(3):
        for row_off in range(3):
            for col_off in range(3):
                window = padded[depth_off:depth_off + depth_total, row_off:row_off + grid_height, col_off:col_off + grid_width].reshape(rows_total, channel_count)
                weights = kernel[depth_off, row_off, col_off]
                response = response + lax.dot_general(window, weights, (((1,), (1,)), ((), ())), preferred_element_type=jnp.float32)
                grad_parts.append(lax.dot_general(flat_grad, window, (((0,), (0,)), ((), ())), preferred_element_type=jnp.float32))
                back_window = grad_padded[2 - depth_off:2 - depth_off + depth_total, 2 - row_off:2 - row_off + grid_height, 2 - col_off:2 - col_off + grid_width].reshape(rows_total, channel_count)
                volume_grad = volume_grad + jnp.dot(back_window, weights, preferred_element_type=jnp.float32)
    shape_out = (depth_total, grid_height, grid_width, channel_count)
    kernel_grad = jnp.stack(grad_parts).reshape(3, 3, 3, channel_count, channel_count) * (rows_total ** -0.5)
    return response.reshape(shape_out).astype(jnp.bfloat16), volume_grad.reshape(shape_out).astype(jnp.bfloat16), kernel_grad
```

```python
import jax
import jax.numpy as jnp
from jax import lax
from jax.sharding import PartitionSpec as P

LANES = 128


def padded_2(block, sides, width):
    for axis, dim in sides:
        count = lax.axis_size(axis)
        forward = [(i, i + 1) for i in range(count - 1)]
        backward = [(target, source) for source, target in forward]
        low = lax.ppermute(
            lax.slice_in_dim(block, block.shape[dim] - width, None, axis=dim), axis, forward
        )
        high = lax.ppermute(lax.slice_in_dim(block, 0, width, axis=dim), axis, backward)
        block = jnp.concatenate([low, block, high], axis=dim)
    return block


def pad_sides(field):
    return jnp.pad(field, ((0, 0), (1, 1), (1, 1), (0, 0)))


def back_window(padded, depth_off, row_off, col_off, plane_count, grid_height, grid_width):
    sliced = padded[
        2 - depth_off : 2 - depth_off + plane_count,
        2 - row_off : 2 - row_off + grid_height,
        2 - col_off : 2 - col_off + grid_width,
    ]
    return sliced.reshape(plane_count * grid_height * grid_width, padded.shape[3])


def gather_by_exchange(block, axis):
    copies = jnp.broadcast_to(block[None], (lax.axis_size(axis),) + block.shape)
    return lax.all_to_all(copies, axis, 0, 0, tiled=True)


def encode(block):
    top = (jnp.max(jnp.abs(block)) * 1.01).astype(jnp.bfloat16)
    scale = jnp.where(top > 0, top, jnp.ones_like(top)).astype(jnp.float32)
    unit = block / scale
    square = unit * unit
    code = jnp.where(unit < 0, -square, square) * square
    return code.astype(jnp.bfloat16).at[-1].set(scale.astype(jnp.bfloat16))


def decode(codes):
    codes = codes.astype(jnp.float32)
    size = jnp.sqrt(jnp.sqrt(jnp.abs(codes))) * codes[:, -1:, :]
    return jnp.where(codes < 0, -size, size)


def sum_everywhere(grad, scale):
    count = lax.axis_size("space")
    rows, columns = grad.shape
    groups = columns // LANES
    lines = rows * groups
    per = -(-(lines + count) // (count * 16)) * 16
    flat = grad.reshape(rows, groups, LANES).transpose(1, 0, 2).reshape(lines, LANES)
    flat = jnp.pad(flat, ((0, count * (per - 1) - lines), (0, 0))).reshape(count, per - 1, LANES)
    flat = jnp.pad(flat, ((0, 0), (0, 1), (0, 0)))
    parts = lax.all_to_all(flat, "space", 0, 0, tiled=True)
    whole = decode(gather_by_exchange(encode(parts.sum(0) * scale), "space"))
    whole = whole[:, :-1].reshape(count * (per - 1), LANES)[:lines]
    return whole.reshape(groups, rows, LANES).transpose(1, 0, 2).reshape(rows, columns)


def per_device(volume, kernel, cotangent):
    plane_count, grid_height, grid_width, local_channels = volume.shape
    rows_local = plane_count * grid_height * grid_width
    filt = lax.axis_size("filt")
    flat_grad = cotangent.reshape(rows_local, local_channels)
    turned = volume.reshape(rows_local, local_channels).T
    gathered = gather_by_exchange(turned, "filt").reshape(filt * local_channels, rows_local).T
    gathered = gathered.reshape(plane_count, grid_height, grid_width, filt * local_channels)
    extended = padded_2(gathered, (("space", 0),), 1)
    response = jnp.zeros((rows_local, local_channels), jnp.float32)
    padded = pad_sides(extended)
    piece_width = extended.shape[3]
    grad_parts = []
    for depth_off in range(3):
        for row_off in range(3):
            for col_off in range(3):
                window = padded[
                    depth_off : depth_off + plane_count,
                    row_off : row_off + grid_height,
                    col_off : col_off + grid_width,
                ].reshape(rows_local, piece_width)
                weights = kernel[depth_off, row_off, col_off]
                response = response + lax.dot_general(
                    window, weights, (((1,), (1,)), ((), ())), preferred_element_type=jnp.float32
                )
                grad_parts.append(
                    lax.dot_general(
                        flat_grad,
                        window,
                        (((0,), (0,)), ((), ())),
                        preferred_element_type=jnp.float32,
                    )
                )
    stacked = jnp.stack(grad_parts).reshape(27 * local_channels, piece_width)
    total_rows = rows_local * lax.axis_size("space")
    kernel_grad = sum_everywhere(stacked, total_rows ** (-0.5))
    kernel_grad = kernel_grad.reshape(3, 3, 3, local_channels, piece_width)
    grad_extended = padded_2(cotangent, (("space", 0),), 1)
    grad_padded = pad_sides(grad_extended)
    total = jnp.zeros((filt * local_channels, rows_local), jnp.float32)
    for depth_off in range(3):
        for row_off in range(3):
            for col_off in range(3):
                weights = kernel[depth_off, row_off, col_off]
                window = back_window(
                    grad_padded, depth_off, row_off, col_off, plane_count, grid_height, grid_width
                )
                total = total + lax.dot_general(
                    weights, window, (((0,), (1,)), ((), ())), preferred_element_type=jnp.float32
                )
    terms = total.reshape(filt, local_channels, rows_local)
    summed = lax.all_to_all(terms, "filt", 0, 0, tiled=True).sum(0)
    volume_grad = summed.T
    shape_out = (plane_count, grid_height, grid_width, local_channels)
    return (
        response.reshape(shape_out).astype(jnp.bfloat16),
        volume_grad.reshape(shape_out).astype(jnp.bfloat16),
        kernel_grad,
    )


def solution(mesh):
    placed = (
        P("space", None, None, "filt"),
        P(None, None, None, "filt", None),
        P("space", None, None, "filt"),
    )
    return jax.shard_map(
        per_device,
        mesh=mesh,
        in_specs=placed,
        out_specs=(
            P("space", None, None, "filt"),
            P("space", None, None, "filt"),
            P(None, None, None, "filt", None),
        ),
        check_vma=False,
    )
```

```python
import jax
import jax.numpy as jnp
from jax import lax
from jax.experimental import pallas as pl
from jax.experimental.pallas import tpu as pltpu
from jax.sharding import Mesh
from jax.sharding import PartitionSpec as P

LANES = 128
F32 = jnp.float32
BF16 = jnp.bfloat16
SPACE = ("x", "y", "z_hi")
FILT = ("z_lo", "core")
VMEM_LIMIT = 48 * 1024 * 1024


def shifted(field, height, width, row, col):
    size = height * width
    step = row * width + col
    moved = field if step == 0 else pltpu.roll(field, (-step) % size, 1)
    if step == 0:
        return moved
    lane = lax.broadcasted_iota(jnp.int32, field.shape, 1)
    at_row = lane // width + row
    at_col = lane % width + col
    inside = (at_row >= 0) & (at_row < height) & (at_col >= 0) & (at_col < width)
    return jnp.where(inside, moved, jnp.zeros_like(moved))


def call(body, out_shape, args, scratch=(), cost=0):
    return pl.pallas_call(
        body,
        out_shape=out_shape,
        in_specs=[pl.BlockSpec(memory_space=pltpu.VMEM)] * len(args),
        out_specs=pl.BlockSpec(memory_space=pltpu.VMEM),
        scratch_shapes=list(scratch),
        compiler_params=pltpu.CompilerParams(vmem_limit_bytes=VMEM_LIMIT),
        cost_estimate=pl.CostEstimate(flops=cost, bytes_accessed=4 << 20, transcendentals=0),
    )(*args)


def response_of(kernel, planes, height, width):
    own, channels = kernel.shape[3:]
    size = height * width

    def body(kernel_ref, low_ref, mid_ref, high_ref, out_ref):
        total = jnp.zeros((9 * own, size), F32)
        for depth, ref in enumerate((low_ref, mid_ref, high_ref)):
            weights = kernel_ref[depth].reshape(9 * own, channels)
            total = total + jnp.dot(weights, ref[...], preferred_element_type=F32)
        result = jnp.zeros((own, size), F32)
        for row in range(3):
            for col in range(3):
                at = (row * 3 + col) * own
                result = result + shifted(total[at : at + own], height, width, row - 1, col - 1)
        out_ref[...] = result

    return call(
        body,
        jax.ShapeDtypeStruct((own, size), F32),
        (kernel, *planes),
        cost=2 * 27 * own * channels * size,
    )


def volume_terms(kernel, grads, height, width):
    own, channels = kernel.shape[3:]
    size = height * width

    def body(kernel_ref, grads_ref, out_ref, patch_ref):
        for depth in range(3):
            plane = grads_ref[depth * own : (depth + 1) * own].astype(F32)
            for row in range(3):
                for col in range(3):
                    at = (depth * 9 + row * 3 + col) * own
                    moved = shifted(plane, height, width, 1 - row, 1 - col)
                    patch_ref[at : at + own] = moved.astype(BF16)
        out_ref[...] = lax.dot_general(
            kernel_ref[...].reshape(27 * own, channels),
            patch_ref[...],
            (((0,), (0,)), ((), ())),
            preferred_element_type=F32,
        )

    return call(
        body,
        jax.ShapeDtypeStruct((channels, size), F32),
        (kernel, grads),
        scratch=[pltpu.VMEM((27 * own, size), BF16)],
        cost=2 * 27 * own * channels * size,
    )


def kernel_terms(parts, own, height, width, lines):
    planes, rows, size = parts.shape
    part = rows - 3 * own
    columns = -(-9 * part // LANES) * LANES

    def body(parts_ref, out_ref, patch_ref):
        patch_ref[9 * part :] = jnp.zeros((columns - 9 * part, planes * size), BF16)
        total = jnp.zeros((3 * own, columns), F32)
        for plane in range(planes):
            lanes = slice(plane * size, (plane + 1) * size)
            field = parts_ref[plane, 3 * own :].astype(F32)
            for row in range(3):
                for col in range(3):
                    at = (row * 3 + col) * part
                    moved = shifted(field, height, width, row - 1, col - 1)
                    patch_ref[at : at + part, lanes] = moved.astype(BF16)
            total = total + lax.dot_general(
                parts_ref[plane, : 3 * own],
                patch_ref[:, lanes],
                (((1,), (1,)), ((), ())),
                preferred_element_type=F32,
            )
        for tile in range(columns // LANES):
            out_ref[tile * 3 * own : (tile + 1) * 3 * own] = total[:, tile * LANES : (tile + 1) * LANES]
        used = columns // LANES * 3 * own
        out_ref[used:] = jnp.zeros((lines - used, LANES), F32)

    return call(
        body,
        jax.ShapeDtypeStruct((lines, LANES), F32),
        (parts,),
        scratch=[pltpu.VMEM((columns, planes * size), BF16)],
        cost=2 * 27 * own * part * size * planes,
    )


def encode(block, used, copies, scale):
    def body(block_ref, out_ref):
        values = block_ref[...] * scale
        top = jnp.max(jnp.max(jnp.abs(values), axis=0, keepdims=True), axis=1, keepdims=True)
        top = (top * 1.01).astype(BF16).astype(F32)
        top = jnp.where(top > 0, top, jnp.ones_like(top))
        unit = values / top
        square = unit * unit
        code = (jnp.where(unit < 0, -square, square) * square).astype(BF16)
        tops = jnp.broadcast_to(top, (block.shape[0] - used, LANES)).astype(BF16)
        for copy in range(copies):
            out_ref[copy] = code
            out_ref[copy, used:] = tops

    return call(body, jax.ShapeDtypeStruct((copies,) + block.shape, BF16), (block,))


def decode(codes, own, part):
    parts = codes.shape[0]
    columns = -(-9 * part // LANES) * LANES
    used = columns // LANES * 3 * own

    def body(codes_ref, out_ref):
        depth = pl.program_id(0)
        pieces = []
        for index in range(parts):
            tiles = [
                codes_ref[index, pl.ds(pl.multiple_of(tile * 3 * own + depth * own, 16), own)]
                for tile in range(columns // LANES)
            ]
            code = jnp.concatenate(tiles, axis=1).astype(F32)
            size = jnp.sqrt(jnp.sqrt(jnp.abs(code))) * codes_ref[index, used : used + 16].astype(F32)[:1, :1]
            pieces.append(jnp.where(code < 0, -size, size))
        for at in range(9):
            out_ref[at] = jnp.concatenate([piece[:, at * part : (at + 1) * part] for piece in pieces], axis=1)

    return pl.pallas_call(
        body,
        grid=(3,),
        out_shape=jax.ShapeDtypeStruct((27, own, parts * part), F32),
        in_specs=[pl.BlockSpec(memory_space=pltpu.VMEM)],
        out_specs=pl.BlockSpec((9, own, parts * part), lambda i: (i, 0, 0)),
        compiler_params=pltpu.CompilerParams(vmem_limit_bytes=VMEM_LIMIT),
        cost_estimate=pl.CostEstimate(flops=1 << 22, bytes_accessed=3 << 20, transcendentals=0),
    )(codes)


def exchange(blocks, axis):
    return lax.all_to_all(blocks, axis, 0, 0, tiled=True)


def copies_of(block, count):
    return jnp.broadcast_to(block[None], (count,) + block.shape)


def per_device(volume, kernel, cotangent):
    planes, height, width, own = volume.shape
    channels = kernel.shape[4]
    size = planes * height * width
    n_x, n_y, n_pair = (lax.axis_size(axis) for axis in SPACE)
    n_space, n_filt = n_x * n_y * n_pair, lax.axis_size(FILT)
    part = channels // n_x

    volume_t = volume.reshape(size, own).T
    grad_t = cotangent.reshape(size, own).T
    both = jnp.concatenate([grad_t, volume_t])
    forward = [(i, i + 1) for i in range(n_space - 1)]
    backward = [(target, source) for source, target in forward]
    low = lax.ppermute(both, SPACE, forward)
    high = lax.ppermute(both, SPACE, backward)
    grads = jnp.concatenate([high[:own], grad_t, low[:own]])

    mid = exchange(copies_of(volume_t, n_filt), FILT).reshape(channels, size)
    sides = jnp.concatenate([low[own:], high[own:]])
    sides = exchange(copies_of(sides, n_filt), FILT).reshape(n_filt, 2, own, size)
    low_plane = sides[:, 0].reshape(channels, size)
    high_plane = sides[:, 1].reshape(channels, size)

    parts = exchange(
        jnp.concatenate([copies_of(grads, n_x), mid.reshape(n_x, part, size)], axis=1), "x"
    )
    tiles = -(-9 * part // LANES)
    used = tiles * 3 * own
    per = -(-(used + 16) // (16 * n_y)) * 16
    terms = kernel_terms(parts, own, height, width, per * n_y)
    block = exchange(terms.reshape(n_y, per, LANES), "y").sum(0)
    for step in range(1, n_pair):
        other = lax.ppermute(block, "z_hi", [(i, (i + step) % n_pair) for i in range(n_pair)])
        total = block + other if step == 1 else total + other
    whole = exchange(copies_of(total, n_y), "y").reshape(n_y * per, LANES)
    codes = exchange(encode(whole, used, n_x, (size * n_space) ** -0.5), "x")
    kernel_grad = decode(codes, own, part).reshape(3, 3, 3, own, channels)

    response = response_of(kernel, (low_plane, mid, high_plane), height, width)
    summands = volume_terms(kernel, grads, height, width).reshape(n_filt, own, size)
    volume_grad = exchange(summands, FILT).sum(0)
    return (
        response.T.astype(BF16).reshape(volume.shape),
        volume_grad.T.astype(BF16).reshape(volume.shape),
        kernel_grad,
    )


def solution(mesh):
    axes = SPACE + FILT
    fine = Mesh(mesh.devices.reshape(4, 8, 2, 4, 2), axes)
    channels_last = P(SPACE, None, None, FILT)
    weights = P(None, None, None, FILT, None)
    return jax.shard_map(
        per_device,
        mesh=fine,
        in_specs=(channels_last, weights, channels_last),
        out_specs=(channels_last, channels_last, weights),
        check_vma=False,
    )
```

```python
import jax
import jax.numpy as jnp
from jax import lax
from jax.experimental import pallas as pl
from jax.experimental.pallas import tpu as pltpu
from jax.sharding import Mesh
from jax.sharding import PartitionSpec as P

LANES = 128
F32 = jnp.float32
BF16 = jnp.bfloat16
SPACE = ("x", "y", "z_hi")
FILT = ("z_lo", "core")
VMEM_LIMIT = 48 * 1024 * 1024


def shifted(field, height, width, row, col):
    size = height * width
    step = row * width + col
    moved = field if step == 0 else pltpu.roll(field, (-step) % size, 1)
    if step == 0:
        return moved
    lane = lax.broadcasted_iota(jnp.int32, field.shape, 1)
    at_row = lane // width + row
    at_col = lane % width + col
    inside = (at_row >= 0) & (at_row < height) & (at_col >= 0) & (at_col < width)
    return jnp.where(inside, moved, jnp.zeros_like(moved))


def call(body, out_shape, args, scratch=(), cost=0):
    return pl.pallas_call(
        body,
        out_shape=out_shape,
        in_specs=[pl.BlockSpec(memory_space=pltpu.VMEM)] * len(args),
        out_specs=pl.BlockSpec(memory_space=pltpu.VMEM),
        scratch_shapes=list(scratch),
        compiler_params=pltpu.CompilerParams(vmem_limit_bytes=VMEM_LIMIT),
        cost_estimate=pl.CostEstimate(flops=cost, bytes_accessed=4 << 20, transcendentals=0),
    )(*args)


def response_of(kernel, planes, height, width):
    own, channels = kernel.shape[3:]
    size = height * width

    def body(kernel_ref, low_ref, mid_ref, high_ref, out_ref):
        total = jnp.zeros((9 * own, size), F32)
        for depth, ref in enumerate((low_ref, mid_ref, high_ref)):
            weights = kernel_ref[depth].reshape(9 * own, channels)
            total = total + jnp.dot(weights, ref[...], preferred_element_type=F32)
        result = jnp.zeros((own, size), F32)
        for row in range(3):
            for col in range(3):
                at = (row * 3 + col) * own
                result = result + shifted(total[at : at + own], height, width, row - 1, col - 1)
        out_ref[...] = result

    return call(
        body,
        jax.ShapeDtypeStruct((own, size), F32),
        (kernel, *planes),
        cost=2 * 27 * own * channels * size,
    )


def volume_terms(kernel, grads, height, width):
    own, channels = kernel.shape[3:]
    size = height * width

    def body(kernel_ref, grads_ref, out_ref, patch_ref):
        for depth in range(3):
            plane = grads_ref[depth * own : (depth + 1) * own].astype(F32)
            for row in range(3):
                for col in range(3):
                    at = (depth * 9 + row * 3 + col) * own
                    moved = shifted(plane, height, width, 1 - row, 1 - col)
                    patch_ref[at : at + own] = moved.astype(BF16)
        out_ref[...] = lax.dot_general(
            kernel_ref[...].reshape(27 * own, channels),
            patch_ref[...],
            (((0,), (0,)), ((), ())),
            preferred_element_type=F32,
        )

    return call(
        body,
        jax.ShapeDtypeStruct((channels, size), F32),
        (kernel, grads),
        scratch=[pltpu.VMEM((27 * own, size), BF16)],
        cost=2 * 27 * own * channels * size,
    )


def pack(fields, grads, count):
    channels, size = fields.shape
    half = grads.shape[0] // 2
    part = channels // (count // 2)
    room = -(-part // 16) * 16

    def body(fields_ref, grads_ref, out_ref):
        wide = grads_ref[...].astype(F32)
        filler = jnp.zeros((room - part, size), F32)
        everything = fields_ref[...].astype(F32)
        for place in range(count):
            index, side = divmod(place, 2)
            rows = [everything[index * part : (index + 1) * part], filler, wide[side * half : (side + 1) * half]]
            out_ref[place] = jnp.concatenate(rows, axis=0).astype(BF16)

    return call(body, jax.ShapeDtypeStruct((count, room + half, size), BF16), (fields, grads))


def kernel_block(parts, part, height, width, copies, scale):
    planes, rows, size = parts.shape
    room = -(-part // 16) * 16
    half = rows - room
    half_room = -(-half // 16) * 16
    used = 27 * half
    tiles = -(-used // LANES)
    group = 8

    def body(parts_ref, out_ref, patch_ref, grads_ref, stack_ref):
        grads_ref[:, : 2 * size] = jnp.zeros((3 * half_room, 2 * size), BF16)
        grads_ref[:, planes * size :] = jnp.zeros((3 * half_room, 2 * size), BF16)

        def spread(plane):
            block = parts_ref[plane].astype(F32)
            lanes = pl.ds(pl.multiple_of(plane * size, size), size)
            for row in range(3):
                for col in range(3):
                    at = (row * 3 + col) * room
                    moved = shifted(block[:room], height, width, row - 1, col - 1)
                    patch_ref[at : at + room, lanes] = moved.astype(BF16)
            filler = jnp.zeros((half_room - half, size), F32)
            field = jnp.concatenate([block[room:], filler], axis=0).astype(BF16)
            for depth in range(3):
                ahead = pl.ds(pl.multiple_of((plane + depth) * size, size), size)
                grads_ref[depth * half_room : (depth + 1) * half_room, ahead] = field

        def some(index, carry):
            for plane in range(group):
                spread(index * group + plane)
            return carry

        lax.fori_loop(0, planes // group, some, 0)
        total = jnp.zeros((9 * room, 3 * half_room), F32)
        for index in range(planes // group):
            lanes = slice(index * group * size, (index + 1) * group * size)
            behind = slice(lanes.start + size, lanes.stop + size)
            total = total + lax.dot_general(
                patch_ref[:, lanes],
                grads_ref[:, behind],
                (((1,), (1,)), ((), ())),
                preferred_element_type=F32,
            )
        pieces = []
        for depth in range(3):
            for at in range(9):
                piece = total[at * room : (at + 1) * room, depth * half_room : depth * half_room + half]
                pieces.append(piece)
        pieces.append(jnp.zeros((room, tiles * LANES - used), F32))
        values = jnp.concatenate(pieces, axis=1) * scale
        top = jnp.max(jnp.max(jnp.abs(values), axis=0, keepdims=True), axis=1, keepdims=True)
        top = (top * 1.01).astype(BF16).astype(F32)
        top = jnp.where(top > 0, top, jnp.ones_like(top))
        unit = values / top
        square = unit * unit
        code = jnp.where(unit < 0, -square, square) * square
        lane = lax.broadcasted_iota(jnp.int32, code.shape, 1)
        code = jnp.where(lane < used, code, jnp.broadcast_to(top, code.shape))
        for tile in range(tiles):
            stack_ref[tile * part : tile * part + room] = code[:, tile * LANES : (tile + 1) * LANES]
        result = stack_ref[: tiles * part].astype(BF16)
        for copy in range(copies):
            out_ref[copy] = result

    return call(
        body,
        jax.ShapeDtypeStruct((copies, tiles * part, LANES), BF16),
        (parts,),
        scratch=[
            pltpu.VMEM((9 * room, planes * size), BF16),
            pltpu.VMEM((3 * half_room, (planes + 2) * size), BF16),
            pltpu.VMEM((tiles * part + room, LANES), F32),
        ],
        cost=2 * 27 * half * part * planes * size,
    )


def decode(codes, own, channels):
    count, lines, _ = codes.shape
    half, part = own // 2, channels // (count // 2)
    tiles = lines // part

    def body(codes_ref, out_ref, wide_ref, stack_ref):
        for place in range(count):
            code = codes_ref[place].astype(F32)
            top = code[lines - 8 :, LANES - 1 :][:1]
            size = jnp.sqrt(jnp.sqrt(jnp.abs(code))) * top
            wide_ref[place] = jnp.where(code < 0, -size, size)
        for side in range(2):
            for tile in range(tiles):
                for index in range(count // 2):
                    piece = wide_ref[2 * index + side, tile * part : (tile + 1) * part]
                    stack_ref[index * part : (index + 1) * part] = piece
                turned = stack_ref[...].T
                at = tile * LANES
                stop = min(at + LANES, 27 * half)
                while at < stop:
                    tap, first = divmod(at, half)
                    many = min(half - first, stop - at)
                    from_row = at - tile * LANES
                    to_row = side * half + first
                    out_ref[tap, to_row : to_row + many] = turned[from_row : from_row + many]
                    at += many

    return call(
        body,
        jax.ShapeDtypeStruct((27, own, channels), F32),
        (codes,),
        scratch=[pltpu.VMEM((count, lines, LANES), F32), pltpu.VMEM((channels, LANES), F32)],
    )


def exchange(blocks, axis):
    return lax.all_to_all(blocks, axis, 0, 0, tiled=True)


def copies_of(block, count):
    return jnp.broadcast_to(block[None], (count,) + block.shape)


def per_device(volume, kernel, cotangent):
    planes, height, width, own = volume.shape
    channels = kernel.shape[4]
    size = planes * height * width
    n_x, n_y, n_pair = (lax.axis_size(axis) for axis in SPACE)
    n_space, n_filt = n_x * n_y * n_pair, lax.axis_size(FILT)
    part = channels // (n_x * n_y)

    volume_t = volume.reshape(size, own).T
    grad_t = cotangent.reshape(size, own).T
    mid = exchange(copies_of(volume_t, n_filt), FILT).reshape(channels, size)
    parts = exchange(pack(mid, grad_t, n_space), SPACE)

    forward = [(i, i + 1) for i in range(n_space - 1)]
    backward = [(target, source) for source, target in forward]
    low_grad, high_grad = (lax.ppermute(grad_t, SPACE, way) for way in (forward, backward))
    grads = jnp.concatenate([high_grad, grad_t, low_grad])
    summands = volume_terms(kernel, grads, height, width)
    volume_grad = lax.psum_scatter(summands, FILT, scatter_dimension=0, tiled=True)
    low_plane, high_plane = (lax.ppermute(mid, SPACE, way) for way in (forward, backward))
    response = response_of(kernel, (low_plane, mid, high_plane), height, width)

    near = n_y * n_pair
    block = kernel_block(parts, part, height, width, near, (size * n_space) ** -0.5)
    line = exchange(block, ("y", "z_hi"))
    codes = exchange(copies_of(line, n_x), "x").reshape((n_space,) + block.shape[1:])
    kernel_grad = decode(codes, own, channels).reshape(kernel.shape)
    return (
        response.T.astype(BF16).reshape(volume.shape),
        volume_grad.T.astype(BF16).reshape(volume.shape),
        kernel_grad,
    )


def solution(mesh):
    axes = SPACE + FILT
    fine = Mesh(mesh.devices.reshape(4, 8, 2, 4, 2), axes)
    channels_last = P(SPACE, None, None, FILT)
    weights = P(None, None, None, FILT, None)
    return jax.shard_map(
        per_device,
        mesh=fine,
        in_specs=(channels_last, weights, channels_last),
        out_specs=(channels_last, channels_last, weights),
        check_vma=False,
    )
```

```python
import jax
import jax.numpy as jnp
from jax import lax
from jax.experimental import pallas as pl
from jax.experimental.pallas import tpu as pltpu
from jax.sharding import Mesh
from jax.sharding import PartitionSpec as P

LANES = 128
F32 = jnp.float32
BF16 = jnp.bfloat16
SPACE = ("x", "y", "z_hi")
FILT = ("z_lo", "core")
VMEM_LIMIT = 48 * 1024 * 1024


def shifted(field, height, width, row, col):
    size = height * width
    step = row * width + col
    moved = field if step == 0 else pltpu.roll(field, (-step) % size, 1)
    if step == 0:
        return moved
    lane = lax.broadcasted_iota(jnp.int32, field.shape, 1)
    at_row = lane // width + row
    at_col = lane % width + col
    inside = (at_row >= 0) & (at_row < height) & (at_col >= 0) & (at_col < width)
    return jnp.where(inside, moved, jnp.zeros_like(moved))


def call(body, out_shape, args, scratch=(), cost=0):
    many = isinstance(out_shape, (list, tuple))
    return pl.pallas_call(
        body,
        out_shape=out_shape,
        in_specs=[pl.BlockSpec(memory_space=pltpu.VMEM)] * len(args),
        out_specs=[pl.BlockSpec(memory_space=pltpu.VMEM)] * len(out_shape)
        if many
        else pl.BlockSpec(memory_space=pltpu.VMEM),
        scratch_shapes=list(scratch),
        compiler_params=pltpu.CompilerParams(vmem_limit_bytes=VMEM_LIMIT),
        cost_estimate=pl.CostEstimate(flops=cost, bytes_accessed=4 << 20, transcendentals=0),
    )(*args)


def turned_copies(field, count):
    def body(field_ref, out_ref):
        turned = field_ref[...].astype(F32).T.astype(BF16)
        for copy in range(count):
            out_ref[copy] = turned

    return call(body, jax.ShapeDtypeStruct((count,) + field.shape[::-1], BF16), (field,))


def response_terms(kernel, plane, height, width):
    own, channels = kernel.shape[3:]
    size = height * width

    def body(kernel_ref, plane_ref, out_ref):
        for depth in range(3):
            weights = kernel_ref[depth].reshape(9 * own, channels)
            total = jnp.dot(weights, plane_ref[...], preferred_element_type=F32)
            result = jnp.zeros((own, size), F32)
            for row in range(3):
                for col in range(3):
                    at = (row * 3 + col) * own
                    result = result + shifted(total[at : at + own], height, width, row - 1, col - 1)
            out_ref[depth] = result

    return call(
        body,
        jax.ShapeDtypeStruct((3, own, size), F32),
        (kernel, plane),
        cost=2 * 27 * own * channels * size,
    )


def volume_terms(kernel, high, mid, low, height, width):
    own, channels = kernel.shape[3:]
    size = height * width

    def body(kernel_ref, high_ref, mid_ref, low_ref, out_ref, patch_ref):
        for depth, ref in enumerate((high_ref, mid_ref, low_ref)):
            plane = ref[...].astype(F32)
            for row in range(3):
                for col in range(3):
                    at = (depth * 9 + row * 3 + col) * own
                    moved = shifted(plane, height, width, 1 - row, 1 - col)
                    patch_ref[at : at + own] = moved.astype(BF16)
        out_ref[...] = lax.dot_general(
            kernel_ref[...].reshape(27 * own, channels),
            patch_ref[...],
            (((0,), (0,)), ((), ())),
            preferred_element_type=F32,
        )

    return call(
        body,
        jax.ShapeDtypeStruct((channels, size), F32),
        (kernel, high, mid, low),
        scratch=[pltpu.VMEM((27 * own, size), BF16)],
        cost=2 * 27 * own * channels * size,
    )


def pack(fields, cotangent, count):
    channels, size = fields.shape
    own = cotangent.shape[1]
    half = own // 2
    part = channels // (count // 2)
    cuts = size // LANES
    rows = cuts * (half + part)

    def body(fields_ref, cotangent_ref, out_ref, again_ref, turned_ref):
        wide = cotangent_ref[...].astype(F32).T
        everything = fields_ref[...].astype(F32)
        again_ref[...] = fields_ref[...]
        turned_ref[...] = wide.astype(BF16)
        for place in range(count):
            index, side = divmod(place, 2)
            pieces = []
            for cut in range(cuts):
                lanes = slice(cut * LANES, (cut + 1) * LANES)
                pieces.append(wide[side * half : (side + 1) * half, lanes])
                pieces.append(everything[index * part : (index + 1) * part, lanes])
            out_ref[place] = jnp.concatenate(pieces, axis=0).astype(BF16)

    return call(
        body,
        [
            jax.ShapeDtypeStruct((count, rows, LANES), BF16),
            jax.ShapeDtypeStruct((channels, size), BF16),
            jax.ShapeDtypeStruct((own, size), BF16),
        ],
        (fields, cotangent),
    )


def kernel_block(parts, passed, half, height, width, copies, scale):
    planes, lines, _ = parts.shape
    size = height * width
    cuts = size // LANES
    rows = lines // cuts
    part = rows - half
    room = -(-part // 16) * 16
    half_room = -(-half // 16) * 16
    used = 27 * half
    tiles = -(-used // LANES)
    group = 8

    def body(parts_ref, passed_ref, out_ref, again_ref, patch_ref, grads_ref, stack_ref):
        again_ref[...] = passed_ref[...]
        grads_ref[:, : 2 * size] = jnp.zeros((3 * half_room, 2 * size), BF16)
        grads_ref[:, planes * size :] = jnp.zeros((3 * half_room, 2 * size), BF16)

        def spread(plane):
            block = parts_ref[plane].astype(F32)
            block = jnp.concatenate([block[cut * rows : (cut + 1) * rows] for cut in range(cuts)], axis=1)
            lanes = pl.ds(pl.multiple_of(plane * size, size), size)
            field = jnp.concatenate([block[half:], jnp.zeros((room - part, size), F32)], axis=0)
            for row in range(3):
                for col in range(3):
                    at = (row * 3 + col) * room
                    moved = shifted(field, height, width, row - 1, col - 1)
                    patch_ref[at : at + room, lanes] = moved.astype(BF16)
            filler = jnp.zeros((half_room - half, size), F32)
            grad = jnp.concatenate([block[:half], filler], axis=0).astype(BF16)
            for depth in range(3):
                ahead = pl.ds(pl.multiple_of((plane + depth) * size, size), size)
                grads_ref[depth * half_room : (depth + 1) * half_room, ahead] = grad

        def some(index, carry):
            for plane in range(group):
                spread(index * group + plane)
            return carry

        lax.fori_loop(0, planes // group, some, 0)
        total = jnp.zeros((9 * room, 3 * half_room), F32)
        for index in range(planes // group):
            lanes = slice(index * group * size, (index + 1) * group * size)
            behind = slice(lanes.start + size, lanes.stop + size)
            total = total + lax.dot_general(
                patch_ref[:, lanes],
                grads_ref[:, behind],
                (((1,), (1,)), ((), ())),
                preferred_element_type=F32,
            )
        pieces = []
        for depth in range(3):
            for at in range(9):
                piece = total[at * room : (at + 1) * room, depth * half_room : depth * half_room + half]
                pieces.append(piece)
        pieces.append(jnp.zeros((room, tiles * LANES - used), F32))
        values = jnp.concatenate(pieces, axis=1) * scale
        top = jnp.max(jnp.max(jnp.abs(values), axis=0, keepdims=True), axis=1, keepdims=True)
        top = (top * 1.01).astype(BF16).astype(F32)
        top = jnp.where(top > 0, top, jnp.ones_like(top))
        unit = values / top
        square = unit * unit
        code = jnp.where(unit < 0, -square, square) * square
        lane = lax.broadcasted_iota(jnp.int32, code.shape, 1)
        code = jnp.where(lane < used, code, jnp.broadcast_to(top, code.shape))
        for tile in range(tiles):
            stack_ref[tile * part : tile * part + room] = code[:, tile * LANES : (tile + 1) * LANES]
        result = stack_ref[: tiles * part].astype(BF16)
        for copy in range(copies):
            out_ref[copy] = result

    return call(
        body,
        [
            jax.ShapeDtypeStruct((copies, tiles * part, LANES), BF16),
            jax.ShapeDtypeStruct(passed.shape, passed.dtype),
        ],
        (parts, passed),
        scratch=[
            pltpu.VMEM((9 * room, planes * size), BF16),
            pltpu.VMEM((3 * half_room, (planes + 2) * size), BF16),
            pltpu.VMEM((tiles * part + room, LANES), F32),
        ],
        cost=2 * 27 * half * part * planes * size,
    )


def decode(codes, own, channels):
    count, lines, _ = codes.shape
    half, part = own // 2, channels // (count // 2)
    tiles = lines // part

    def body(codes_ref, out_ref, wide_ref, stack_ref):
        for place in range(count):
            code = codes_ref[place].astype(F32)
            top = code[lines - 8 :, LANES - 1 :][:1]
            size = jnp.sqrt(jnp.sqrt(jnp.abs(code))) * top
            wide_ref[place] = jnp.where(code < 0, -size, size)
        for side in range(2):
            for tile in range(tiles):
                for index in range(count // 2):
                    piece = wide_ref[2 * index + side, tile * part : (tile + 1) * part]
                    stack_ref[index * part : (index + 1) * part] = piece
                turned = stack_ref[...].T
                at = tile * LANES
                stop = min(at + LANES, 27 * half)
                while at < stop:
                    tap, first = divmod(at, half)
                    many = min(half - first, stop - at)
                    from_row = at - tile * LANES
                    to_row = side * half + first
                    out_ref[tap, to_row : to_row + many] = turned[from_row : from_row + many]
                    at += many

    return call(
        body,
        jax.ShapeDtypeStruct((27, own, channels), F32),
        (codes,),
        scratch=[pltpu.VMEM((count, lines, LANES), F32), pltpu.VMEM((channels, LANES), F32)],
    )


def exchange(blocks, axis):
    return lax.all_to_all(blocks, axis, 0, 0, tiled=True)


def copies_of(block, count):
    return jnp.broadcast_to(block[None], (count,) + block.shape)


def per_device(volume, kernel, cotangent):
    planes, height, width, own = volume.shape
    channels = kernel.shape[4]
    size = planes * height * width
    n_x, n_y, n_pair = (lax.axis_size(axis) for axis in SPACE)
    n_z, n_core = (lax.axis_size(axis) for axis in FILT)
    n_space, n_filt = n_x * n_y * n_pair, n_z * n_core

    mid = exchange(turned_copies(volume.reshape(size, own), n_filt), FILT).reshape(channels, size)
    packed, mid, grad = pack(mid, cotangent.reshape(size, own), n_space)
    parts = exchange(packed, SPACE)

    forward = [(i, i + 1) for i in range(n_space - 1)]
    backward = [(target, source) for source, target in forward]
    low_grad = lax.ppermute(grad, SPACE, forward)
    high_grad = lax.ppermute(grad, SPACE, backward)
    terms = response_terms(kernel, mid, height, width)
    response = terms[1] + lax.ppermute(terms[0], SPACE, forward)
    response = response + lax.ppermute(terms[2], SPACE, backward)

    summands = volume_terms(kernel, high_grad, grad, low_grad, height, width)
    summands = summands.reshape(n_z, n_core, own, size)
    core = lax.axis_index("core")
    keep = lax.dynamic_index_in_dim(summands, core, 1, keepdims=False)
    give = lax.dynamic_index_in_dim(summands, 1 - core, 1, keepdims=False)
    sums = keep + lax.ppermute(give, "core", [(0, 1), (1, 0)])

    near = n_y * n_pair
    block, sums = kernel_block(parts, sums, own // 2, height, width, near, (size * n_space) ** -0.5)
    line = exchange(block, ("y", "z_hi"))
    place = lax.axis_index("z_lo")
    volume_grad = lax.dynamic_index_in_dim(sums, place, 0, keepdims=False)
    for step in range(1, n_z):
        give = lax.dynamic_index_in_dim(sums, (place + step) % n_z, 0, keepdims=False)
        ring = [(i, (i + step) % n_z) for i in range(n_z)]
        volume_grad = volume_grad + lax.ppermute(give, "z_lo", ring)

    codes = exchange(copies_of(line, n_x), "x").reshape((n_space,) + block.shape[1:])
    kernel_grad = decode(codes, own, channels).reshape(kernel.shape)
    return (
        response.T.astype(BF16).reshape(volume.shape),
        volume_grad.T.astype(BF16).reshape(volume.shape),
        kernel_grad,
    )


def solution(mesh):
    axes = SPACE + FILT
    fine = Mesh(mesh.devices.reshape(4, 8, 2, 4, 2), axes)
    channels_last = P(SPACE, None, None, FILT)
    weights = P(None, None, None, FILT, None)
    return jax.shard_map(
        per_device,
        mesh=fine,
        in_specs=(channels_last, weights, channels_last),
        out_specs=(channels_last, channels_last, weights),
        check_vma=False,
    )
```

```python
import jax
import jax.numpy as jnp
from jax import lax
from jax.experimental import pallas as pl
from jax.experimental.pallas import tpu as pltpu
from jax.sharding import Mesh
from jax.sharding import PartitionSpec as P

LANES = 128
F32 = jnp.float32
BF16 = jnp.bfloat16
SPACE = ("x", "y", "z_hi")
FILT = ("z_lo", "core")
VMEM_LIMIT = 48 * 1024 * 1024


def shifted(field, height, width, row, col):
    size = height * width
    step = row * width + col
    moved = field if step == 0 else pltpu.roll(field, (-step) % size, 1)
    if step == 0:
        return moved
    lane = lax.broadcasted_iota(jnp.int32, field.shape, 1)
    at_row = lane // width + row
    at_col = lane % width + col
    inside = (at_row >= 0) & (at_row < height) & (at_col >= 0) & (at_col < width)
    return jnp.where(inside, moved, jnp.zeros_like(moved))


def call(body, out_shape, args, scratch=(), cost=0, scalar=None, after=()):
    many = isinstance(out_shape, (list, tuple))
    whole = pl.BlockSpec(memory_space=pltpu.VMEM)
    in_specs, operands = [whole] * len(args), list(args)
    run = body
    if scalar is not None:
        in_specs = [pl.BlockSpec(memory_space=pltpu.SMEM)] + in_specs
        operands = [scalar.reshape(1)] + operands
    if after:
        in_specs = [pl.BlockSpec(memory_space=pl.ANY)] * len(after) + in_specs
        operands = list(after) + operands

        def run(*refs):
            body(*refs[len(after) :])

    return pl.pallas_call(
        run,
        out_shape=out_shape,
        in_specs=in_specs,
        out_specs=[whole] * len(out_shape) if many else whole,
        scratch_shapes=list(scratch),
        compiler_params=pltpu.CompilerParams(vmem_limit_bytes=VMEM_LIMIT),
        cost_estimate=pl.CostEstimate(flops=cost, bytes_accessed=4 << 20, transcendentals=0),
    )(*operands)


def turn(volume, cotangent, count):
    def body(volume_ref, cotangent_ref, copies_ref, turned_ref):
        turned = volume_ref[...].astype(F32).T.astype(BF16)
        for copy in range(count):
            copies_ref[copy] = turned
        turned_ref[...] = cotangent_ref[...].astype(F32).T.astype(BF16)

    shape = volume.shape[::-1]
    return call(
        body,
        [jax.ShapeDtypeStruct((count,) + shape, BF16), jax.ShapeDtypeStruct(shape, BF16)],
        (volume, cotangent),
    )


def response_terms(kernel, plane, grad, height, width, after):
    own, channels = kernel.shape[3:]
    size = height * width

    def body(kernel_ref, plane_ref, grad_ref, next_ref, before_ref, out_ref):
        wide = grad_ref[...].astype(F32)
        next_ref[:own] = wide
        before_ref[:own] = wide
        for depth, ref in enumerate((next_ref, out_ref, before_ref)):
            weights = kernel_ref[depth].reshape(9 * own, channels)
            total = jnp.dot(weights, plane_ref[...], preferred_element_type=F32)
            result = jnp.zeros((own, size), F32)
            for row in range(3):
                for col in range(3):
                    at = (row * 3 + col) * own
                    result = result + shifted(total[at : at + own], height, width, row - 1, col - 1)
            if depth == 1:
                ref[...] = result
            else:
                ref[own:] = result

    both = jax.ShapeDtypeStruct((2 * own, size), F32)
    return call(
        body,
        [both, both, jax.ShapeDtypeStruct((own, size), F32)],
        (kernel, plane, grad),
        cost=2 * 27 * own * channels * size,
        after=after,
    )


def volume_terms(kernel, high, mid, low, height, width, core, n_core, after):
    own, channels = kernel.shape[3:]
    size = height * width
    groups = channels // own // n_core

    def body(core_ref, kernel_ref, high_ref, mid_ref, low_ref, keep_ref, give_ref, patch_ref):
        for depth, ref in enumerate((high_ref, mid_ref, low_ref)):
            plane = ref[:own].astype(F32)
            for row in range(3):
                for col in range(3):
                    at = (depth * 9 + row * 3 + col) * own
                    moved = shifted(plane, height, width, 1 - row, 1 - col)
                    patch_ref[at : at + own] = moved.astype(BF16)
        result = lax.dot_general(
            kernel_ref[...].reshape(27 * own, channels),
            patch_ref[...],
            (((0,), (0,)), ((), ())),
            preferred_element_type=F32,
        )
        first = core_ref[0] == 0
        for group in range(groups):
            at = group * n_core * own
            even, odd = result[at : at + own], result[at + own : at + 2 * own]
            keep_ref[group] = jnp.where(first, even, odd)
            give_ref[group] = jnp.where(first, odd, even)

    half = jax.ShapeDtypeStruct((groups, own, size), F32)
    return call(
        body,
        [half, half],
        (kernel, high, mid, low),
        scratch=[pltpu.VMEM((27 * own, size), BF16)],
        cost=2 * 27 * own * channels * size,
        scalar=core,
        after=after,
    )


def pack(fields, grads, count):
    channels, size = fields.shape
    half = grads.shape[0] // 2
    part = channels // (count // 2)
    cuts = size // LANES
    rows = cuts * (half + part)

    def body(fields_ref, grads_ref, out_ref):
        wide = grads_ref[...].astype(F32)
        everything = fields_ref[...].astype(F32)
        for place in range(count):
            index, side = divmod(place, 2)
            pieces = []
            for cut in range(cuts):
                lanes = slice(cut * LANES, (cut + 1) * LANES)
                pieces.append(wide[side * half : (side + 1) * half, lanes])
                pieces.append(everything[index * part : (index + 1) * part, lanes])
            out_ref[place] = jnp.concatenate(pieces, axis=0).astype(BF16)

    return call(body, jax.ShapeDtypeStruct((count, rows, LANES), BF16), (fields, grads))


def kernel_block(parts, half, height, width, copies, scale, after):
    planes, lines, _ = parts.shape
    size = height * width
    cuts = size // LANES
    rows = lines // cuts
    part = rows - half
    room = -(-part // 16) * 16
    half_room = -(-half // 16) * 16
    used = 27 * half
    tiles = -(-used // LANES)
    group = 8

    def body(parts_ref, out_ref, patch_ref, grads_ref, stack_ref):
        grads_ref[:, : 2 * size] = jnp.zeros((3 * half_room, 2 * size), BF16)
        grads_ref[:, planes * size :] = jnp.zeros((3 * half_room, 2 * size), BF16)

        def spread(plane):
            block = parts_ref[plane].astype(F32)
            block = jnp.concatenate([block[cut * rows : (cut + 1) * rows] for cut in range(cuts)], axis=1)
            lanes = pl.ds(pl.multiple_of(plane * size, size), size)
            field = jnp.concatenate([block[half:], jnp.zeros((room - part, size), F32)], axis=0)
            for row in range(3):
                for col in range(3):
                    at = (row * 3 + col) * room
                    moved = shifted(field, height, width, row - 1, col - 1)
                    patch_ref[at : at + room, lanes] = moved.astype(BF16)
            filler = jnp.zeros((half_room - half, size), F32)
            grad = jnp.concatenate([block[:half], filler], axis=0).astype(BF16)
            for depth in range(3):
                ahead = pl.ds(pl.multiple_of((plane + depth) * size, size), size)
                grads_ref[depth * half_room : (depth + 1) * half_room, ahead] = grad

        def some(index, carry):
            for plane in range(group):
                spread(index * group + plane)
            return carry

        lax.fori_loop(0, planes // group, some, 0)
        total = jnp.zeros((9 * room, 3 * half_room), F32)
        for index in range(planes // group):
            lanes = slice(index * group * size, (index + 1) * group * size)
            behind = slice(lanes.start + size, lanes.stop + size)
            total = total + lax.dot_general(
                patch_ref[:, lanes],
                grads_ref[:, behind],
                (((1,), (1,)), ((), ())),
                preferred_element_type=F32,
            )
        pieces = []
        for depth in range(3):
            for at in range(9):
                piece = total[at * room : (at + 1) * room, depth * half_room : depth * half_room + half]
                pieces.append(piece)
        pieces.append(jnp.zeros((room, tiles * LANES - used), F32))
        values = jnp.concatenate(pieces, axis=1) * scale
        top = jnp.max(jnp.max(jnp.abs(values), axis=0, keepdims=True), axis=1, keepdims=True)
        top = (top * 1.01).astype(BF16).astype(F32)
        top = jnp.where(top > 0, top, jnp.ones_like(top))
        unit = values / top
        square = unit * unit
        code = jnp.where(unit < 0, -square, square) * square
        lane = lax.broadcasted_iota(jnp.int32, code.shape, 1)
        code = jnp.where(lane < used, code, jnp.broadcast_to(top, code.shape))
        for tile in range(tiles):
            stack_ref[tile * part : tile * part + room] = code[:, tile * LANES : (tile + 1) * LANES]
        result = stack_ref[: tiles * part].astype(BF16)
        for copy in range(copies):
            out_ref[copy] = result

    return call(
        body,
        jax.ShapeDtypeStruct((copies, tiles * part, LANES), BF16),
        (parts,),
        scratch=[
            pltpu.VMEM((9 * room, planes * size), BF16),
            pltpu.VMEM((3 * half_room, (planes + 2) * size), BF16),
            pltpu.VMEM((tiles * part + room, LANES), F32),
        ],
        cost=2 * 27 * half * part * planes * size,
        after=after,
    )


def decode(codes, own, channels):
    count, lines, _ = codes.shape
    half, part = own // 2, channels // (count // 2)
    tiles = lines // part

    def body(codes_ref, out_ref, wide_ref, stack_ref):
        for place in range(count):
            code = codes_ref[place].astype(F32)
            top = code[lines - 8 :, LANES - 1 :][:1]
            size = jnp.sqrt(jnp.sqrt(jnp.abs(code))) * top
            wide_ref[place] = jnp.where(code < 0, -size, size)
        for side in range(2):
            for tile in range(tiles):
                for index in range(count // 2):
                    piece = wide_ref[2 * index + side, tile * part : (tile + 1) * part]
                    stack_ref[index * part : (index + 1) * part] = piece
                turned = stack_ref[...].T
                at = tile * LANES
                stop = min(at + LANES, 27 * half)
                while at < stop:
                    tap, first = divmod(at, half)
                    many = min(half - first, stop - at)
                    from_row = at - tile * LANES
                    to_row = side * half + first
                    out_ref[tap, to_row : to_row + many] = turned[from_row : from_row + many]
                    at += many

    return call(
        body,
        jax.ShapeDtypeStruct((27, own, channels), F32),
        (codes,),
        scratch=[pltpu.VMEM((count, lines, LANES), F32), pltpu.VMEM((channels, LANES), F32)],
    )


def share(line, copies, response, low, high, keep, got, place):
    own, size = response.shape
    groups = keep.shape[0]

    def body(place_ref, line_ref, response_ref, low_ref, high_ref, keep_ref, got_ref, lines_ref, out_ref, *sums):
        for copy in range(copies):
            lines_ref[copy] = line_ref[...]
        total = response_ref[...] + low_ref[own:] + high_ref[own:]
        out_ref[...] = total.T.astype(BF16)
        both = [keep_ref[group] + got_ref[group] for group in range(groups)]
        for step, ref in enumerate(sums):
            picked = both[step]
            for at in range(1, groups):
                picked = jnp.where(place_ref[0] == at, both[(at + step) % groups], picked)
            ref[...] = picked

    piece = jax.ShapeDtypeStruct((own, size), F32)
    lines, out, *pieces = call(
        body,
        [jax.ShapeDtypeStruct((copies,) + line.shape, BF16), jax.ShapeDtypeStruct((size, own), BF16)]
        + [piece] * groups,
        (line, response, low, high, keep, got),
        scalar=place,
    )
    return lines, out, pieces


def sum_turned(parts):
    own, size = parts[0].shape

    def body(*refs):
        total = refs[0][...]
        for ref in refs[1:-1]:
            total = total + ref[...]
        refs[-1][...] = total.T.astype(BF16)

    return call(body, jax.ShapeDtypeStruct((size, own), BF16), parts)


def exchange(blocks, axis):
    return lax.all_to_all(blocks, axis, 0, 0, tiled=True)


def per_device(volume, kernel, cotangent):
    planes, height, width, own = volume.shape
    channels = kernel.shape[4]
    size = planes * height * width
    n_x, n_y, n_pair = (lax.axis_size(axis) for axis in SPACE)
    n_z, n_core = (lax.axis_size(axis) for axis in FILT)
    n_space, n_filt = n_x * n_y * n_pair, n_z * n_core

    copies, grad = turn(volume.reshape(size, own), cotangent.reshape(size, own), n_filt)
    mid = exchange(copies, FILT).reshape(channels, size)
    packed = pack(mid, grad, n_space)
    parts = exchange(packed, SPACE)

    forward = [(i, i + 1) for i in range(n_space - 1)]
    backward = [(target, source) for source, target in forward]
    to_next, to_before, response = response_terms(kernel, mid, grad, height, width, (packed,))
    low = lax.ppermute(to_next, SPACE, forward)
    high = lax.ppermute(to_before, SPACE, backward)

    near = n_y * n_pair
    block = kernel_block(parts, own // 2, height, width, near, (size * n_space) ** -0.5, (low, high))
    line = exchange(block, ("y", "z_hi"))

    core = lax.axis_index("core")
    keep, give = volume_terms(kernel, high, grad, low, height, width, core, n_core, (block,))
    got = lax.ppermute(give, "core", [(i, n_core - 1 - i) for i in range(n_core)])

    lines, response, pieces = share(line, n_x, response, low, high, keep, got, lax.axis_index("z_lo"))
    codes = exchange(lines, "x").reshape((n_space,) + block.shape[1:])
    for step in range(1, n_z):
        pieces[step] = lax.ppermute(pieces[step], "z_lo", [(i, (i + step) % n_z) for i in range(n_z)])
    volume_grad = sum_turned(pieces)
    kernel_grad = decode(codes, own, channels).reshape(kernel.shape)
    return response.reshape(volume.shape), volume_grad.reshape(volume.shape), kernel_grad


def solution(mesh):
    axes = SPACE + FILT
    fine = Mesh(mesh.devices.reshape(4, 8, 2, 4, 2), axes)
    channels_last = P(SPACE, None, None, FILT)
    weights = P(None, None, None, FILT, None)
    return jax.shard_map(
        per_device,
        mesh=fine,
        in_specs=(channels_last, weights, channels_last),
        out_specs=(channels_last, channels_last, weights),
        check_vma=False,
    )
```

```python
import jax
import jax.numpy as jnp
from jax import lax
from jax.experimental import pallas as pl
from jax.experimental.pallas import tpu as pltpu
from jax.sharding import Mesh
from jax.sharding import PartitionSpec as P

LANES = 128
F32 = jnp.float32
BF16 = jnp.bfloat16
SPACE = ("x", "y", "z_hi")
FILT = ("z_lo", "core")
VMEM_LIMIT = 48 * 1024 * 1024


def shifted(field, height, width, row, col):
    size = height * width
    step = row * width + col
    moved = field if step == 0 else pltpu.roll(field, (-step) % size, 1)
    if step == 0:
        return moved
    lane = lax.broadcasted_iota(jnp.int32, field.shape, 1)
    at_row = lane // width + row
    at_col = lane % width + col
    inside = (at_row >= 0) & (at_row < height) & (at_col >= 0) & (at_col < width)
    return jnp.where(inside, moved, jnp.zeros_like(moved))


def call(body, out_shape, args, scratch=(), cost=0, scalar=None, after=()):
    many = isinstance(out_shape, (list, tuple))
    whole = pl.BlockSpec(memory_space=pltpu.VMEM)
    in_specs, operands = [whole] * len(args), list(args)
    run = body
    if scalar is not None:
        in_specs = [pl.BlockSpec(memory_space=pltpu.SMEM)] + in_specs
        operands = [scalar.reshape(-1)] + operands
    if after:
        in_specs = [pl.BlockSpec(memory_space=pl.ANY)] * len(after) + in_specs
        operands = list(after) + operands

        def run(*refs):
            body(*refs[len(after) :])

    return pl.pallas_call(
        run,
        out_shape=out_shape,
        in_specs=in_specs,
        out_specs=[whole] * len(out_shape) if many else whole,
        scratch_shapes=list(scratch),
        compiler_params=pltpu.CompilerParams(vmem_limit_bytes=VMEM_LIMIT),
        cost_estimate=pl.CostEstimate(flops=cost, bytes_accessed=4 << 20, transcendentals=0),
    )(*operands)


def turn(volume, cotangent, count):
    def body(volume_ref, cotangent_ref, copies_ref, turned_ref):
        turned = volume_ref[...].astype(F32).T.astype(BF16)
        for copy in range(count):
            copies_ref[copy] = turned
        turned_ref[...] = cotangent_ref[...].astype(F32).T.astype(BF16)

    shape = volume.shape[::-1]
    return call(
        body,
        [jax.ShapeDtypeStruct((count,) + shape, BF16), jax.ShapeDtypeStruct(shape, BF16)],
        (volume, cotangent),
    )


def response_terms(kernel, plane, height, width, after):
    own, channels = kernel.shape[3:]
    size = height * width

    def body(kernel_ref, plane_ref, next_ref, out_ref, before_ref):
        for depth, ref in enumerate((next_ref, out_ref, before_ref)):
            weights = kernel_ref[depth].reshape(9 * own, channels)
            total = jnp.dot(weights, plane_ref[...], preferred_element_type=F32)
            result = jnp.zeros((own, size), F32)
            for row in range(3):
                for col in range(3):
                    at = (row * 3 + col) * own
                    result = result + shifted(total[at : at + own], height, width, row - 1, col - 1)
            ref[...] = result

    return call(
        body,
        [jax.ShapeDtypeStruct((own, size), F32)] * 3,
        (kernel, plane),
        cost=2 * 27 * own * channels * size,
        after=after,
    )


def volume_terms(kernel, own_parts, height, width, pair, core, n_core, after):
    own, channels = kernel.shape[3:]
    size = height * width
    groups = channels // own // n_core

    def body(places_ref, kernel_ref, parts_ref, keep_ref, give_ref, patch_ref):
        even = places_ref[0] == 0
        wide = parts_ref[:, own:].astype(F32)
        mine, beyond = wide[:, :own], wide[:, own:]
        high = jnp.where(even, mine[1], beyond[0])
        mid = jnp.where(even, mine[0], mine[1])
        low = jnp.where(even, beyond[1], mine[0])
        for depth, plane in enumerate((high, mid, low)):
            for row in range(3):
                for col in range(3):
                    at = (depth * 9 + row * 3 + col) * own
                    moved = shifted(plane, height, width, 1 - row, 1 - col)
                    patch_ref[at : at + own] = moved.astype(BF16)
        result = lax.dot_general(
            kernel_ref[...].reshape(27 * own, channels),
            patch_ref[...],
            (((0,), (0,)), ((), ())),
            preferred_element_type=F32,
        )
        first = places_ref[1] == 0
        for group in range(groups):
            at = group * n_core * own
            one, two = result[at : at + own], result[at + own : at + 2 * own]
            keep_ref[group] = jnp.where(first, one, two)
            give_ref[group] = jnp.where(first, two, one)

    half = jax.ShapeDtypeStruct((groups, own, size), F32)
    return call(
        body,
        [half, half],
        (kernel, own_parts),
        scratch=[pltpu.VMEM((27 * own, size), BF16)],
        cost=2 * 27 * own * channels * size,
        scalar=jnp.stack([pair, core]),
        after=after,
    )


def pack(fields, grad, beyond):
    count, part, size = fields.shape
    own = grad.shape[0]

    def body(fields_ref, grad_ref, beyond_ref, out_ref):
        for place in range(count):
            out_ref[place, :part] = fields_ref[place]
            out_ref[place, part : part + own] = grad_ref[...]
            out_ref[place, part + own :] = beyond_ref[...]

    return call(body, jax.ShapeDtypeStruct((count, part + 2 * own, size), BF16), (fields, grad, beyond))


def kernel_terms(parts, own, height, width, chunks, after):
    planes, rows, size = parts.shape
    part = rows - 2 * own
    used = 27 * own
    tiles = -(-used // LANES)
    piece = part // chunks
    lines = -(-(tiles * piece + 1) // 8) * 8

    def body(parts_ref, out_ref, patch_ref, grads_ref, wide_ref):
        for plane in range(planes):
            lanes = slice(plane * size, (plane + 1) * size)
            field = parts_ref[plane, :part].astype(F32)
            for row in range(3):
                for col in range(3):
                    at = (row * 3 + col) * part
                    moved = shifted(field, height, width, row - 1, col - 1)
                    patch_ref[at : at + part, lanes] = moved.astype(BF16)
        for first in range(0, planes, 2):
            mine = [parts_ref[first + side, part : part + own] for side in range(2)]
            beyond = [parts_ref[first + side, part + own :] for side in range(2)]
            for side, grads in enumerate(((mine[1], mine[0], beyond[1]), (beyond[0], mine[1], mine[0]))):
                lanes = slice((first + side) * size, (first + side + 1) * size)
                for depth, grad in enumerate(grads):
                    grads_ref[depth * own : (depth + 1) * own, lanes] = grad
        total = lax.dot_general(
            patch_ref[...], grads_ref[...], (((1,), (1,)), ((), ())), preferred_element_type=F32
        )
        pieces = [total[at * part : (at + 1) * part] for at in range(9)]
        pieces.append(jnp.zeros((part, tiles * LANES - used), F32))
        wide_ref[...] = jnp.concatenate(pieces, axis=1)
        for chunk in range(chunks):
            rows_of = slice(chunk * piece, (chunk + 1) * piece)
            for tile in range(tiles):
                lanes = slice(tile * LANES, (tile + 1) * LANES)
                out_ref[chunk, tile * piece : (tile + 1) * piece] = wide_ref[rows_of, lanes]
            out_ref[chunk, tiles * piece :] = jnp.zeros((lines - tiles * piece, LANES), F32)

    return call(
        body,
        jax.ShapeDtypeStruct((chunks, lines, LANES), F32),
        (parts,),
        scratch=[
            pltpu.VMEM((9 * part, planes * size), BF16),
            pltpu.VMEM((3 * own, planes * size), BF16),
            pltpu.VMEM((part, tiles * LANES), F32),
        ],
        cost=2 * 27 * own * part * planes * size,
        after=after,
    )


def add_encode(parts, copies, scale, after):
    _, lines, _ = parts.shape

    def body(parts_ref, out_ref):
        values = parts_ref[0]
        for at in range(1, parts.shape[0]):
            values = values + parts_ref[at]
        values = values * scale
        top = jnp.max(jnp.max(jnp.abs(values), axis=0, keepdims=True), axis=1, keepdims=True)
        top = (top * 1.01).astype(BF16).astype(F32)
        top = jnp.where(top > 0, top, jnp.ones_like(top))
        unit = values / top
        square = unit * unit
        code = jnp.where(unit < 0, -square, square) * square
        row = lax.broadcasted_iota(jnp.int32, code.shape, 0)
        code = jnp.where(row < lines - 1, code, jnp.broadcast_to(top, code.shape)).astype(BF16)
        for copy in range(copies):
            out_ref[copy] = code

    return call(body, jax.ShapeDtypeStruct((copies, lines, LANES), BF16), (parts,), after=after)


def decode(codes, own, channels, order):
    count, lines, _ = codes.shape
    piece = channels // count
    used = 27 * own
    tiles = -(-used // LANES)

    def body(codes_ref, out_ref, wide_ref, stack_ref):
        for place in range(count):
            code = codes_ref[place].astype(F32)
            size = jnp.sqrt(jnp.sqrt(jnp.abs(code))) * code[lines - 8 :][7:, :1]
            wide_ref[place] = jnp.where(code < 0, -size, size)
        for tile in range(tiles):
            for at, place in enumerate(order):
                stack_ref[at * piece : (at + 1) * piece] = wide_ref[place, tile * piece : (tile + 1) * piece]
            turned = stack_ref[...].T
            at = tile * LANES
            stop = min(at + LANES, used)
            while at < stop:
                tap, first = divmod(at, own)
                many = min(own - first, stop - at)
                window, depth = divmod(tap, 3)
                from_row = at - tile * LANES
                out_ref[depth * 9 + window, first : first + many] = turned[from_row : from_row + many]
                at += many

    return call(
        body,
        jax.ShapeDtypeStruct((27, own, channels), F32),
        (codes,),
        scratch=[pltpu.VMEM((count, lines, LANES), F32), pltpu.VMEM((channels, LANES), F32)],
    )


def sums_by_place(keep, got, place, after):
    groups = keep.shape[0]

    def body(place_ref, keep_ref, got_ref, *refs):
        both = [keep_ref[group] + got_ref[group] for group in range(groups)]
        for step, ref in enumerate(refs):
            picked = both[step]
            for at in range(1, groups):
                picked = jnp.where(place_ref[0] == at, both[(at + step) % groups], picked)
            ref[...] = picked

    piece = jax.ShapeDtypeStruct(keep.shape[1:], F32)
    return list(call(body, [piece] * groups, (keep, got), scalar=place, after=after))


def finish(line, copies, halves):
    own, size = halves[0][0].shape

    def body(line_ref, *refs):
        terms, (lines_ref, *outs) = refs[: -len(halves) - 1], refs[-len(halves) - 1 :]
        for copy in range(copies):
            lines_ref[copy] = line_ref[...]
        for half, out in zip(halves, outs, strict=True):
            total = terms[0][...]
            for ref in terms[1 : len(half)]:
                total = total + ref[...]
            terms = terms[len(half) :]
            out[...] = total.T.astype(BF16)

    done = jax.ShapeDtypeStruct((size, own), BF16)
    return call(
        body,
        [jax.ShapeDtypeStruct((copies,) + line.shape, BF16)] + [done] * len(halves),
        (line, *(term for half in halves for term in half)),
    )


def exchange(blocks, axis):
    return lax.all_to_all(blocks, axis, 0, 0, tiled=True)


def per_device(volume, kernel, cotangent):
    planes, height, width, own = volume.shape
    channels = kernel.shape[4]
    size = planes * height * width
    n_x, n_y, n_pair = (lax.axis_size(axis) for axis in SPACE)
    n_z, n_core = (lax.axis_size(axis) for axis in FILT)
    n_space, n_filt = n_x * n_y * n_pair, n_z * n_core


    copies, grad = turn(volume.reshape(size, own), cotangent.reshape(size, own), n_filt)
    beyond = [(i, i - 2) for i in range(2, n_space, 2)] + [(i, i + 2) for i in range(1, n_space - 2, 2)]
    beyond = lax.ppermute(grad, SPACE, beyond)
    mid = exchange(copies, FILT)
    packed = pack(mid, grad, beyond)
    parts = exchange(packed, ("x", "z_hi"))

    forward = [(i, i + 1) for i in range(n_space - 1)]
    backward = [(target, source) for source, target in forward]
    to_next, response, to_before = response_terms(kernel, mid.reshape(channels, size), height, width, (packed,))
    low = lax.ppermute(to_next, SPACE, forward)
    high = lax.ppermute(to_before, SPACE, backward)

    terms = kernel_terms(parts, own, height, width, n_y, (low, high))

    pair, core = lax.axis_index("z_hi"), lax.axis_index("core")
    own_parts = lax.dynamic_slice_in_dim(parts, lax.axis_index("x") * n_pair, n_pair, 0)
    keep, give = volume_terms(kernel, own_parts, height, width, pair, core, n_core, (terms,))
    got = lax.ppermute(give, "core", [(i, n_core - 1 - i) for i in range(n_core)])

    terms = exchange(terms, "y")
    block = add_encode(terms, n_y * n_pair, (size * n_space) ** -0.5, (got,))
    line = exchange(block, ("y", "z_hi"))
    pieces = sums_by_place(keep, got, lax.axis_index("z_lo"), (block,))
    for step in range(1, n_z):
        pieces[step] = lax.ppermute(pieces[step], "z_lo", [(i, (i + step) % n_z) for i in range(n_z)])

    lines, response, volume_grad = finish(line, n_x, ((response, low, high), pieces))
    codes = exchange(lines, "x").reshape((n_space,) + block.shape[1:])
    order = [(x * n_y + y) * n_pair + z for x in range(n_x) for z in range(n_pair) for y in range(n_y)]
    kernel_grad = decode(codes, own, channels, order).reshape(kernel.shape)
    return response.reshape(volume.shape), volume_grad.reshape(volume.shape), kernel_grad


def solution(mesh):
    axes = SPACE + FILT
    fine = Mesh(mesh.devices.reshape(4, 8, 2, 4, 2), axes)
    channels_last = P(SPACE, None, None, FILT)
    weights = P(None, None, None, FILT, None)
    return jax.shard_map(
        per_device,
        mesh=fine,
        in_specs=(channels_last, weights, channels_last),
        out_specs=(channels_last, channels_last, weights),
        check_vma=False,
    )
```

```python
import jax
import jax.numpy as jnp
from jax import lax
from jax.experimental import pallas as pl
from jax.experimental.pallas import tpu as pltpu
from jax.sharding import Mesh
from jax.sharding import PartitionSpec as P

LANES = 128
F32 = jnp.float32
BF16 = jnp.bfloat16
SPACE = ("x", "y", "z_hi")
FILT = ("z_lo", "core")
VMEM_LIMIT = 48 * 1024 * 1024


def shifted(field, height, width, row, col):
    size = height * width
    step = row * width + col
    moved = field if step == 0 else pltpu.roll(field, (-step) % size, 1)
    if step == 0:
        return moved
    lane = lax.broadcasted_iota(jnp.int32, field.shape, 1)
    at_row = lane // width + row
    at_col = lane % width + col
    inside = (at_row >= 0) & (at_row < height) & (at_col >= 0) & (at_col < width)
    return jnp.where(inside, moved, jnp.zeros_like(moved))


def call(body, out_shape, args, scratch=(), cost=0, scalar=None, after=()):
    many = isinstance(out_shape, (list, tuple))
    whole = pl.BlockSpec(memory_space=pltpu.VMEM)
    in_specs, operands = [whole] * len(args), list(args)
    run = body
    if scalar is not None:
        in_specs = [pl.BlockSpec(memory_space=pltpu.SMEM)] + in_specs
        operands = [scalar.reshape(-1)] + operands
    if after:
        in_specs = [pl.BlockSpec(memory_space=pl.ANY)] * len(after) + in_specs
        operands = list(after) + operands

        def run(*refs):
            body(*refs[len(after) :])

    return pl.pallas_call(
        run,
        out_shape=out_shape,
        in_specs=in_specs,
        out_specs=[whole] * len(out_shape) if many else whole,
        scratch_shapes=list(scratch),
        compiler_params=pltpu.CompilerParams(vmem_limit_bytes=VMEM_LIMIT),
        cost_estimate=pl.CostEstimate(flops=cost, bytes_accessed=4 << 20, transcendentals=0),
    )(*operands)


TOKEN = jax.ShapeDtypeStruct((8, LANES), F32)


def turn(volume, cotangent, count):
    def body(volume_ref, cotangent_ref, copies_ref, turned_ref, first_ref, second_ref, sems):
        first = pltpu.make_async_copy(volume_ref, first_ref, sems.at[0])
        second = pltpu.make_async_copy(cotangent_ref, second_ref, sems.at[1])
        first.start()
        second.start()
        first.wait()
        turned = first_ref[...].astype(F32).T.astype(BF16)
        for copy in range(count):
            copies_ref[copy] = turned
        second.wait()
        turned_ref[...] = second_ref[...].astype(F32).T.astype(BF16)

    shape = volume.shape[::-1]
    return pl.pallas_call(
        body,
        out_shape=[jax.ShapeDtypeStruct((count,) + shape, BF16), jax.ShapeDtypeStruct(shape, BF16)],
        in_specs=[pl.BlockSpec(memory_space=pltpu.HBM)] * 2,
        out_specs=[pl.BlockSpec(memory_space=pltpu.VMEM)] * 2,
        scratch_shapes=[
            pltpu.VMEM(volume.shape, BF16),
            pltpu.VMEM(cotangent.shape, BF16),
            pltpu.SemaphoreType.DMA((2,)),
        ],
        compiler_params=pltpu.CompilerParams(vmem_limit_bytes=VMEM_LIMIT),
    )(volume, cotangent)


def response_terms(kernel, plane, height, width, pair, after):
    own, channels = kernel.shape[3:]
    size = height * width

    def body(pair_ref, kernel_ref, plane_ref, outside_ref, inside_ref, out_ref):
        results = []
        for depth in range(3):
            weights = kernel_ref[depth].reshape(9 * own, channels)
            total = jnp.dot(weights, plane_ref[...], preferred_element_type=F32)
            result = jnp.zeros((own, size), F32)
            for row in range(3):
                for col in range(3):
                    at = (row * 3 + col) * own
                    result = result + shifted(total[at : at + own], height, width, row - 1, col - 1)
            results.append(result)
        following, out_ref[...], before = results
        even = pair_ref[0] == 0
        outside_ref[...] = jnp.where(even, before, following)
        inside_ref[...] = jnp.where(even, following, before)

    return call(
        body,
        [jax.ShapeDtypeStruct((own, size), F32)] * 3,
        (kernel, plane),
        cost=2 * 27 * own * channels * size,
        scalar=pair,
        after=after,
    )


def volume_terms(kernel, own_parts, height, width, pair, core, n_core, after):
    own, channels = kernel.shape[3:]
    size = height * width
    groups = channels // own // n_core

    def body(places_ref, kernel_ref, parts_ref, keep_ref, give_ref, patch_ref):
        even = places_ref[0] == 0
        wide = parts_ref[:, own:].astype(F32)
        mine, beyond = wide[:, :own], wide[:, own:]
        high = jnp.where(even, mine[1], beyond[0])
        mid = jnp.where(even, mine[0], mine[1])
        low = jnp.where(even, beyond[1], mine[0])
        for depth, plane in enumerate((high, mid, low)):
            for row in range(3):
                for col in range(3):
                    at = (depth * 9 + row * 3 + col) * own
                    moved = shifted(plane, height, width, 1 - row, 1 - col)
                    patch_ref[at : at + own] = moved.astype(BF16)
        result = lax.dot_general(
            kernel_ref[...].reshape(27 * own, channels),
            patch_ref[...],
            (((0,), (0,)), ((), ())),
            preferred_element_type=F32,
        )
        first = places_ref[1] == 0
        for group in range(groups):
            at = group * n_core * own
            one, two = result[at : at + own], result[at + own : at + 2 * own]
            keep_ref[group] = jnp.where(first, one, two)
            give_ref[group] = jnp.where(first, two, one)

    half = jax.ShapeDtypeStruct((groups, own, size), F32)
    return call(
        body,
        [half, half],
        (kernel, own_parts),
        scratch=[pltpu.VMEM((27 * own, size), BF16)],
        cost=2 * 27 * own * channels * size,
        scalar=jnp.stack([pair, core]),
        after=after,
    )


def pack(fields, grad, beyond):
    count, part, size = fields.shape
    own = grad.shape[0]

    def body(fields_ref, grad_ref, beyond_ref, out_ref, token_ref):
        token_ref[...] = jnp.zeros(TOKEN.shape, F32)
        for place in range(count):
            out_ref[place, :part] = fields_ref[place]
            out_ref[place, part : part + own] = grad_ref[...]
            out_ref[place, part + own :] = beyond_ref[...]

    return call(
        body, [jax.ShapeDtypeStruct((count, part + 2 * own, size), BF16), TOKEN], (fields, grad, beyond)
    )


def lines_of(own, piece):
    tiles, over = divmod(27 * own, LANES)
    assert 0 < over and over * piece <= LANES
    return -(-(tiles * piece + 2) // 16) * 16


def kernel_terms(parts, own, height, width, chunks, after):
    planes, rows, size = parts.shape
    part = rows - 2 * own
    used = 27 * own
    tiles, over = divmod(used, LANES)
    piece = part // chunks
    lines = lines_of(own, piece)

    def body(parts_ref, out_ref, token_ref, patch_ref, grads_ref, wide_ref, rest_ref):
        token_ref[...] = jnp.zeros(TOKEN.shape, F32)
        for plane in range(planes):
            lanes = slice(plane * size, (plane + 1) * size)
            field = parts_ref[plane, :part].astype(F32)
            for row in range(3):
                for col in range(3):
                    at = (row * 3 + col) * part
                    moved = shifted(field, height, width, row - 1, col - 1)
                    patch_ref[at : at + part, lanes] = moved.astype(BF16)
        for first in range(0, planes, 2):
            mine = [parts_ref[first + side, part : part + own] for side in range(2)]
            beyond = [parts_ref[first + side, part + own :] for side in range(2)]
            for side, grads in enumerate(((mine[1], mine[0], beyond[1]), (beyond[0], mine[1], mine[0]))):
                lanes = slice((first + side) * size, (first + side + 1) * size)
                for depth, grad in enumerate(grads):
                    grads_ref[depth * own : (depth + 1) * own, lanes] = grad
        total = lax.dot_general(
            patch_ref[...], grads_ref[...], (((1,), (1,)), ((), ())), preferred_element_type=F32
        )
        pieces = [total[at * part : (at + 1) * part] for at in range(9)]
        pieces.append(jnp.zeros((part, LANES - over), F32))
        wide_ref[...] = jnp.concatenate(pieces, axis=1)
        for chunk in range(chunks):
            rows_of = slice(chunk * piece, (chunk + 1) * piece)
            for tile in range(tiles):
                lanes = slice(tile * LANES, (tile + 1) * LANES)
                out_ref[chunk, tile * piece : (tile + 1) * piece] = wide_ref[rows_of, lanes]
            out_ref[chunk, tiles * piece :] = jnp.zeros((lines - tiles * piece, LANES), F32)
        rest_ref[...] = wide_ref[:, tiles * LANES :]
        rest = [rest_ref[pl.ds(at, chunks, stride=piece)][:, :over] for at in range(piece)]
        rest = jnp.concatenate(rest + [jnp.zeros((chunks, LANES - piece * over), F32)], axis=1)
        for chunk in range(chunks):
            out_ref[chunk, tiles * piece : tiles * piece + 1] = rest[chunk : chunk + 1]

    return call(
        body,
        [jax.ShapeDtypeStruct((chunks, lines, LANES), F32), TOKEN],
        (parts,),
        scratch=[
            pltpu.VMEM((9 * part, planes * size), BF16),
            pltpu.VMEM((3 * own, planes * size), BF16),
            pltpu.VMEM((part, (tiles + 1) * LANES), F32),
            pltpu.VMEM((part, LANES), F32),
        ],
        cost=2 * 27 * own * part * planes * size,
        after=after,
    )


def add_encode(parts, copies, scale, after):
    _, lines, _ = parts.shape

    def body(parts_ref, out_ref, token_ref):
        token_ref[...] = jnp.zeros(TOKEN.shape, F32)
        values = parts_ref[0]
        for at in range(1, parts.shape[0]):
            values = values + parts_ref[at]
        values = values * scale
        top = jnp.max(jnp.max(jnp.abs(values), axis=0, keepdims=True), axis=1, keepdims=True)
        top = (top * 1.01).astype(BF16).astype(F32)
        top = jnp.where(top > 0, top, jnp.ones_like(top))
        unit = values / top
        square = unit * unit
        code = jnp.where(unit < 0, -square, square) * square
        row = lax.broadcasted_iota(jnp.int32, code.shape, 0)
        code = jnp.where(row < lines - 1, code, jnp.broadcast_to(top, code.shape)).astype(BF16)
        for copy in range(copies):
            out_ref[copy] = code

    return call(body, [jax.ShapeDtypeStruct((copies, lines, LANES), BF16), TOKEN], (parts,), after=after)


def decode(codes, own, channels, order):
    count, lines, _ = codes.shape
    piece = channels // count
    tiles, over = divmod(27 * own, LANES)
    places = [first + at * stride for first, many, stride in order for at in range(many)]

    def body(codes_ref, out_ref, wide_ref, stack_ref, rest_ref):
        for place in range(count):
            code = codes_ref[place].astype(F32)
            size = lax.rsqrt(lax.rsqrt(jnp.abs(code))) * code[lines - 8 :][7:, :1]
            value = jnp.where(code < 0, -size, size)
            wide_ref[place] = value
            rest_ref[place : place + 1] = value[tiles * piece : tiles * piece + 1]
        for tile in range(tiles + 1):
            if tile < tiles:
                for at, place in enumerate(places):
                    stack_ref[at * piece : (at + 1) * piece] = wide_ref[place, tile * piece : (tile + 1) * piece]
            else:
                rows = [rest_ref[pl.ds(first, many, stride=stride)] for first, many, stride in order]
                rows = jnp.concatenate(rows, axis=0)
                for at in range(piece):
                    moved = pltpu.roll(rows, (LANES - at * over) % LANES, 1) if at else rows
                    stack_ref[pl.ds(at, count, stride=piece)] = moved
            turned = stack_ref[...].T
            at = tile * LANES
            stop = min(at + LANES, 27 * own)
            while at < stop:
                tap, first = divmod(at, own)
                many = min(own - first, stop - at)
                window, depth = divmod(tap, 3)
                from_row = at - tile * LANES
                out_ref[depth * 9 + window, first : first + many] = turned[from_row : from_row + many]
                at += many

    return call(
        body,
        jax.ShapeDtypeStruct((27, own, channels), F32),
        (codes,),
        scratch=[
            pltpu.VMEM((count, lines, LANES), F32),
            pltpu.VMEM((channels, LANES), F32),
            pltpu.VMEM((count, LANES), F32),
        ],
    )


def add(one, two, after):
    def body(one_ref, two_ref, out_ref):
        out_ref[...] = one_ref[...] + two_ref[...]

    return call(body, jax.ShapeDtypeStruct(one.shape, one.dtype), (one, two), after=after)


def sums_by_place(keep, got, place, after):
    groups = keep.shape[0]

    def body(place_ref, keep_ref, got_ref, *refs):
        both = [keep_ref[group] + got_ref[group] for group in range(groups)]
        for step, ref in enumerate(refs):
            picked = both[step]
            for at in range(1, groups):
                picked = jnp.where(place_ref[0] == at, both[(at + step) % groups], picked)
            ref[...] = picked

    piece = jax.ShapeDtypeStruct(keep.shape[1:], F32)
    return list(call(body, [piece] * groups, (keep, got), scalar=place, after=after))


def finish(line, copies, terms):
    own, size = terms[0].shape

    def body(line_ref, *refs):
        terms_refs, (lines_ref, out_ref, token_ref) = refs[:-3], refs[-3:]
        token_ref[...] = jnp.zeros(TOKEN.shape, F32)
        for copy in range(copies):
            lines_ref[copy] = line_ref[...]
        total = terms_refs[0][...]
        for ref in terms_refs[1:]:
            total = total + ref[...]
        out_ref[...] = total.T.astype(BF16)

    return call(
        body,
        [
            jax.ShapeDtypeStruct((copies,) + line.shape, BF16),
            jax.ShapeDtypeStruct((size, own), BF16),
            TOKEN,
        ],
        (line, *terms),
    )


def sum_turned(parts):
    own, size = parts[0].shape

    def body(*refs):
        total = refs[0][...]
        for ref in refs[1:-1]:
            total = total + ref[...]
        refs[-1][...] = total.T.astype(BF16)

    return call(body, jax.ShapeDtypeStruct((size, own), BF16), parts)


def exchange(blocks, axis):
    return lax.all_to_all(blocks, axis, 0, 0, tiled=True)


def per_device(volume, kernel, cotangent):
    planes, height, width, own = volume.shape
    channels = kernel.shape[4]
    size = planes * height * width
    n_x, n_y, n_pair = (lax.axis_size(axis) for axis in SPACE)
    n_z, n_core = (lax.axis_size(axis) for axis in FILT)
    n_space, n_filt = n_x * n_y * n_pair, n_z * n_core


    pair, core, place = (lax.axis_index(axis) for axis in ("z_hi", "core", "z_lo"))
    outside = [(i, i - 2) for i in range(2, n_space, 2)] + [(i, i + 2) for i in range(1, n_space - 2, 2)]

    copies, grad = turn(volume.reshape(size, own), cotangent.reshape(size, own), n_filt)
    beyond = lax.ppermute(grad, SPACE, outside)
    mid = exchange(copies, FILT)
    packed, token = pack(mid, grad, beyond)
    parts = exchange(packed, ("x", "z_hi"))

    far, near, response = response_terms(kernel, mid.reshape(channels, size), height, width, pair, (token,))
    far = lax.ppermute(far, SPACE, outside)

    terms, token = kernel_terms(parts, own, height, width, n_y, (far,))
    own_parts = lax.dynamic_slice_in_dim(parts, lax.axis_index("x") * n_pair, n_pair, 0)
    keep, give = volume_terms(kernel, own_parts, height, width, pair, core, n_core, (token,))
    got = lax.ppermute(give, "core", [(i, n_core - 1 - i) for i in range(n_core)])
    terms = exchange(terms, "y")

    block, token = add_encode(terms, n_y * n_pair, (size * n_space) ** -0.5, (got,))
    line = exchange(block, ("y", "z_hi"))
    pieces = sums_by_place(keep, got, place, (token,))
    for step in range(1, n_z):
        pieces[step] = lax.ppermute(pieces[step], "z_lo", [(i, (i + step) % n_z) for i in range(n_z)])

    lines, volume_grad, token = finish(line, n_x, pieces)
    codes = exchange(lines, "x").reshape((n_space,) + block.shape[1:])
    near = lax.ppermute(add(near, far, (token,)), "z_hi", [(0, 1), (1, 0)])
    response = sum_turned((response, near))
    order = [(x * n_y * n_pair + z, n_y, n_pair) for x in range(n_x) for z in range(n_pair)]
    kernel_grad = decode(codes, own, channels, order).reshape(kernel.shape)
    return response.reshape(volume.shape), volume_grad.reshape(volume.shape), kernel_grad


def solution(mesh):
    axes = SPACE + FILT
    fine = Mesh(mesh.devices.reshape(4, 8, 2, 4, 2), axes)
    channels_last = P(SPACE, None, None, FILT)
    weights = P(None, None, None, FILT, None)
    return jax.shard_map(
        per_device,
        mesh=fine,
        in_specs=(channels_last, weights, channels_last),
        out_specs=(channels_last, channels_last, weights),
        check_vma=False,
    )
```

```python
import jax
import jax.numpy as jnp
from jax import lax
from jax.experimental import pallas as pl
from jax.experimental.pallas import tpu as pltpu
from jax.sharding import Mesh
from jax.sharding import PartitionSpec as P

LANES = 128
F32 = jnp.float32
BF16 = jnp.bfloat16
SPACE = ("x", "y", "z_hi")
FILT = ("z_lo", "core")
VMEM_LIMIT = 48 * 1024 * 1024


def shifted(field, height, width, row, col):
    size = height * width
    step = row * width + col
    moved = field if step == 0 else pltpu.roll(field, (-step) % size, 1)
    if step == 0:
        return moved
    lane = lax.broadcasted_iota(jnp.int32, field.shape, 1)
    at_row = lane // width + row
    at_col = lane % width + col
    inside = (at_row >= 0) & (at_row < height) & (at_col >= 0) & (at_col < width)
    return jnp.where(inside, moved, jnp.zeros_like(moved))


def call(body, out_shape, args, scratch=(), cost=0, scalar=None, after=()):
    many = isinstance(out_shape, (list, tuple))
    whole = pl.BlockSpec(memory_space=pltpu.VMEM)
    in_specs, operands = [whole] * len(args), list(args)
    run = body
    if scalar is not None:
        in_specs = [pl.BlockSpec(memory_space=pltpu.SMEM)] + in_specs
        operands = [scalar.reshape(-1)] + operands
    if after:
        in_specs = [pl.BlockSpec(memory_space=pl.ANY)] * len(after) + in_specs
        operands = list(after) + operands

        def run(*refs):
            body(*refs[len(after) :])

    return pl.pallas_call(
        run,
        out_shape=out_shape,
        in_specs=in_specs,
        out_specs=[whole] * len(out_shape) if many else whole,
        scratch_shapes=list(scratch),
        compiler_params=pltpu.CompilerParams(vmem_limit_bytes=VMEM_LIMIT),
        cost_estimate=pl.CostEstimate(flops=cost, bytes_accessed=4 << 20, transcendentals=0),
    )(*operands)


TOKEN = jax.ShapeDtypeStruct((8, LANES), F32)


def turn(volume, cotangent, count):
    def body(volume_ref, cotangent_ref, copies_ref, turned_ref, first_ref, second_ref, sems):
        first = pltpu.make_async_copy(volume_ref, first_ref, sems.at[0])
        second = pltpu.make_async_copy(cotangent_ref, second_ref, sems.at[1])
        first.start()
        second.start()
        first.wait()
        turned = first_ref[...].astype(F32).T.astype(BF16)
        for copy in range(count):
            copies_ref[copy] = turned
        second.wait()
        turned_ref[...] = second_ref[...].astype(F32).T.astype(BF16)

    shape = volume.shape[::-1]
    return pl.pallas_call(
        body,
        out_shape=[jax.ShapeDtypeStruct((count,) + shape, BF16), jax.ShapeDtypeStruct(shape, BF16)],
        in_specs=[pl.BlockSpec(memory_space=pltpu.HBM)] * 2,
        out_specs=[pl.BlockSpec(memory_space=pltpu.VMEM)] * 2,
        scratch_shapes=[
            pltpu.VMEM(volume.shape, BF16),
            pltpu.VMEM(cotangent.shape, BF16),
            pltpu.SemaphoreType.DMA((2,)),
        ],
        compiler_params=pltpu.CompilerParams(vmem_limit_bytes=VMEM_LIMIT),
    )(*(pltpu.with_memory_space_constraint(array, pltpu.HBM) for array in (volume, cotangent)))


def response_terms(kernel, planes, height, width, pair, after):
    own, channels = kernel.shape[3:]
    size = height * width

    def body(pair_ref, kernel_ref, planes_ref, here_ref, far_ref):
        even = pair_ref[0] == 0
        mine = jnp.where(even, planes_ref[0], planes_ref[1])
        other = jnp.where(even, planes_ref[1], planes_ref[0])
        results = []
        for depth, plane in enumerate((other, mine, other)):
            weights = kernel_ref[depth].reshape(9 * own, channels)
            total = jnp.dot(weights, plane, preferred_element_type=F32)
            result = jnp.zeros((own, size), F32)
            for row in range(3):
                for col in range(3):
                    at = (row * 3 + col) * own
                    result = result + shifted(total[at : at + own], height, width, row - 1, col - 1)
            results.append(result)
        here_ref[...] = results[1] + jnp.where(even, results[2], results[0])
        far_ref[...] = jnp.where(even, results[0], results[2])

    return call(
        body,
        [jax.ShapeDtypeStruct((own, size), F32)] * 2,
        (kernel, planes),
        cost=2 * 27 * own * channels * size,
        scalar=pair,
        after=after,
    )


def volume_terms(kernel, grad, near, height, width, pair, core, n_core, after):
    own, channels = kernel.shape[3:]
    size = height * width
    groups = channels // own // n_core

    def body(places_ref, kernel_ref, grad_ref, near_ref, keep_ref, give_ref, patch_ref):
        even = places_ref[0] == 0
        mid = grad_ref[...].astype(F32)
        inside, outside = near_ref[:own].astype(F32), near_ref[own:].astype(F32)
        high = jnp.where(even, inside, outside)
        low = jnp.where(even, outside, inside)
        for depth, plane in enumerate((high, mid, low)):
            for row in range(3):
                for col in range(3):
                    at = (depth * 9 + row * 3 + col) * own
                    moved = shifted(plane, height, width, 1 - row, 1 - col)
                    patch_ref[at : at + own] = moved.astype(BF16)
        result = lax.dot_general(
            kernel_ref[...].reshape(27 * own, channels),
            patch_ref[...],
            (((0,), (0,)), ((), ())),
            preferred_element_type=F32,
        )
        first = places_ref[1] == 0
        for group in range(groups):
            at = group * n_core * own
            one, two = result[at : at + own], result[at + own : at + 2 * own]
            keep_ref[group] = jnp.where(first, one, two)
            give_ref[group] = jnp.where(first, two, one)

    half = jax.ShapeDtypeStruct((groups, own, size), F32)
    return call(
        body,
        [half, half],
        (kernel, grad, near),
        scratch=[pltpu.VMEM((27 * own, size), BF16)],
        cost=2 * 27 * own * channels * size,
        scalar=jnp.stack([pair, core]),
        after=after,
    )


def stack(one, two):
    rows = one.shape[0]

    def body(one_ref, two_ref, out_ref):
        out_ref[:rows] = one_ref[...]
        out_ref[rows:] = two_ref[...]

    return call(body, jax.ShapeDtypeStruct((rows + two.shape[0], one.shape[1]), one.dtype), (one, two))


def pack(fields, grad, beyond, near, count, pair):
    _, channels, size = fields.shape
    own, part = grad.shape[0], channels // count

    def body(pair_ref, fields_ref, grad_ref, beyond_ref, near_ref, out_ref, token_ref):
        token_ref[...] = jnp.zeros(TOKEN.shape, F32)
        even = pair_ref[0] == 0
        mine, outer = grad_ref[...], beyond_ref[...]
        other, other_outer = near_ref[:own], near_ref[own:]
        grads = [
            jnp.where(even, outer, other_outer),
            jnp.where(even, other, mine),
            jnp.where(even, mine, other),
            jnp.where(even, other_outer, outer),
        ]
        for place in range(count):
            for side in range(2):
                out_ref[place, side * part : (side + 1) * part] = fields_ref[side, place * part : (place + 1) * part]
            for at, plane in enumerate(grads):
                first = 2 * part + at * own
                out_ref[place, first : first + own] = plane

    return call(
        body,
        [jax.ShapeDtypeStruct((count, 2 * part + 4 * own, size), BF16), TOKEN],
        (fields, grad, beyond, near),
        scalar=pair,
    )


def lines_of(own, piece):
    tiles, over = divmod(27 * own, LANES)
    shared = LANES // over
    rest = -(-piece // shared)
    return tiles, over, shared, rest, -(-(tiles * piece + rest + 1) // 16) * 16


def kernel_terms(parts, own, height, width, chunks, after):
    pairs, rows, size = parts.shape
    part = (rows - 4 * own) // 2
    used = 27 * own
    piece = part // chunks
    tiles, over, shared, rest_rows, lines = lines_of(own, piece)

    def body(parts_ref, out_ref, token_ref, patch_ref, grads_ref, wide_ref, rest_ref):
        token_ref[...] = jnp.zeros(TOKEN.shape, F32)
        for at in range(pairs):
            for side in range(2):
                lanes = slice((at * 2 + side) * size, (at * 2 + side + 1) * size)
                field = parts_ref[at, side * part : (side + 1) * part].astype(F32)
                for row in range(3):
                    for col in range(3):
                        first = (row * 3 + col) * part
                        moved = shifted(field, height, width, row - 1, col - 1)
                        patch_ref[first : first + part, lanes] = moved.astype(BF16)
                first = 2 * part + (1 - side) * own
                grads_ref[:, lanes] = parts_ref[at, first : first + 3 * own]
        total = lax.dot_general(
            patch_ref[...], grads_ref[...], (((1,), (1,)), ((), ())), preferred_element_type=F32
        )
        pieces = [total[at * part : (at + 1) * part] for at in range(9)]
        pieces.append(jnp.zeros((part, LANES - over), F32))
        wide_ref[...] = jnp.concatenate(pieces, axis=1)
        rest_ref[...] = wide_ref[:, tiles * LANES :]
        rests = []
        for first in range(0, piece, shared):
            many = min(shared, piece - first)
            rest = [rest_ref[pl.ds(first + at, chunks, stride=piece)][:, :over] for at in range(many)]
            if many * over < LANES:
                rest.append(jnp.zeros((chunks, LANES - many * over), F32))
            rests.append(jnp.concatenate(rest, axis=1))
        for chunk in range(chunks):
            rows_of = slice(chunk * piece, (chunk + 1) * piece)
            for tile in range(tiles):
                lanes = slice(tile * LANES, (tile + 1) * LANES)
                out_ref[chunk, tile * piece : (tile + 1) * piece] = wide_ref[rows_of, lanes]
            out_ref[chunk, tiles * piece :] = jnp.zeros((lines - tiles * piece, LANES), F32)
            for at, rest in enumerate(rests):
                out_ref[chunk, tiles * piece + at : tiles * piece + at + 1] = rest[chunk : chunk + 1]

    return call(
        body,
        [jax.ShapeDtypeStruct((chunks, lines, LANES), F32), TOKEN],
        (parts,),
        scratch=[
            pltpu.VMEM((9 * part, pairs * 2 * size), BF16),
            pltpu.VMEM((3 * own, pairs * 2 * size), BF16),
            pltpu.VMEM((part, (tiles + 1) * LANES), F32),
            pltpu.VMEM((part, LANES), F32),
        ],
        cost=2 * 27 * own * part * pairs * 2 * size,
        after=after,
    )


def add_encode(parts, copies, scale, after):
    _, lines, _ = parts.shape

    def body(parts_ref, out_ref, token_ref):
        token_ref[...] = jnp.zeros(TOKEN.shape, F32)
        values = parts_ref[0]
        for at in range(1, parts.shape[0]):
            values = values + parts_ref[at]
        values = values * scale
        top = jnp.max(jnp.max(jnp.abs(values), axis=0, keepdims=True), axis=1, keepdims=True)
        top = (top * 1.01).astype(BF16).astype(F32)
        top = jnp.where(top > 0, top, jnp.ones_like(top))
        unit = values / top
        square = unit * unit
        code = jnp.where(unit < 0, -square, square) * square
        row = lax.broadcasted_iota(jnp.int32, code.shape, 0)
        code = jnp.where(row < lines - 1, code, jnp.broadcast_to(top, code.shape)).astype(BF16)
        for copy in range(copies):
            out_ref[copy] = code

    return call(body, [jax.ShapeDtypeStruct((copies, lines, LANES), BF16), TOKEN], (parts,), after=after)


def decode(codes, own, channels):
    count, lines, _ = codes.shape
    piece = channels // count
    tiles, over, shared, rest_rows, _ = lines_of(own, piece)

    def body(codes_ref, out_ref, wide_ref, stack_ref, rest_ref):
        for place in range(count):
            code = codes_ref[place].astype(F32)
            size = lax.rsqrt(lax.rsqrt(jnp.abs(code))) * code[lines - 8 :][7:, :1]
            value = jnp.where(code < 0, -size, size)
            wide_ref[place] = value
            for at in range(rest_rows):
                rest_ref[at, place : place + 1] = value[tiles * piece + at : tiles * piece + at + 1]
        for tile in range(tiles + 1):
            if tile < tiles:
                for place in range(count):
                    rows = slice(tile * piece, (tile + 1) * piece)
                    stack_ref[place * piece : (place + 1) * piece] = wide_ref[place, rows]
            else:
                for at in range(piece):
                    row, step = divmod(at, shared)
                    moved = pltpu.roll(rest_ref[row], LANES - step * over, 1) if step else rest_ref[row]
                    stack_ref[pl.ds(at, count, stride=piece)] = moved
            turned = stack_ref[...].T
            at = tile * LANES
            stop = min(at + LANES, 27 * own)
            while at < stop:
                tap, first = divmod(at, own)
                many = min(own - first, stop - at)
                window, depth = divmod(tap, 3)
                from_row = at - tile * LANES
                out_ref[depth * 9 + window, first : first + many] = turned[from_row : from_row + many]
                at += many

    return call(
        body,
        jax.ShapeDtypeStruct((27, own, channels), F32),
        (codes,),
        scratch=[
            pltpu.VMEM((count, lines, LANES), F32),
            pltpu.VMEM((channels, LANES), F32),
            pltpu.VMEM((rest_rows, count, LANES), F32),
        ],
    )


def hand_on(array, after):
    def body(array_ref, out_ref):
        out_ref[...] = array_ref[...]

    return call(body, jax.ShapeDtypeStruct(array.shape, array.dtype), (array,), after=after)


def sums_by_place(keep, got, place, after):
    groups = keep.shape[0]

    def body(place_ref, keep_ref, got_ref, *refs):
        both = [keep_ref[group] + got_ref[group] for group in range(groups)]
        for step, ref in enumerate(refs):
            picked = both[step]
            for at in range(1, groups):
                picked = jnp.where(place_ref[0] == at, both[(at + step) % groups], picked)
            ref[...] = picked

    piece = jax.ShapeDtypeStruct(keep.shape[1:], F32)
    return list(call(body, [piece] * groups, (keep, got), scalar=place, after=after))


def finish(line, copies, terms):
    own, size = terms[0].shape

    def body(line_ref, *refs):
        terms_refs, (lines_ref, out_ref, token_ref) = refs[:-3], refs[-3:]
        token_ref[...] = jnp.zeros(TOKEN.shape, F32)
        for copy in range(copies):
            lines_ref[copy] = line_ref[...]
        total = terms_refs[0][...]
        for ref in terms_refs[1:]:
            total = total + ref[...]
        out_ref[...] = total.T.astype(BF16)

    return call(
        body,
        [
            jax.ShapeDtypeStruct((copies,) + line.shape, BF16),
            jax.ShapeDtypeStruct((size, own), BF16),
            TOKEN,
        ],
        (line, *terms),
    )


def sum_turned(parts):
    own, size = parts[0].shape

    def body(*refs):
        total = refs[0][...]
        for ref in refs[1:-1]:
            total = total + ref[...]
        refs[-1][...] = total.T.astype(BF16)

    return call(body, jax.ShapeDtypeStruct((size, own), BF16), parts)


def exchange(blocks, axis):
    return lax.all_to_all(blocks, axis, 0, 0, tiled=True)


def per_device(volume, kernel, cotangent):
    planes, height, width, own = volume.shape
    channels = kernel.shape[4]
    size = planes * height * width
    n_x, n_y, n_pair = (lax.axis_size(axis) for axis in SPACE)
    n_z, n_core = (lax.axis_size(axis) for axis in FILT)
    n_space, n_filt = n_x * n_y * n_pair, n_z * n_core


    pair, core, place = (lax.axis_index(axis) for axis in ("z_hi", "core", "z_lo"))
    outward = [(i, i - 2) for i in range(2, n_space, 2)] + [(i, i + 2) for i in range(1, n_space - 2, 2)]
    inward = [(target, source) for source, target in outward]
    swap = [(0, 1), (1, 0)]

    copies, grad = turn(volume.reshape(size, own), cotangent.reshape(size, own), n_pair * n_filt)
    beyond = lax.ppermute(grad, SPACE, outward)
    mid = exchange(copies, ("z_hi",) + FILT).reshape(n_pair, channels, size)
    near = lax.ppermute(stack(grad, beyond), "z_hi", swap)
    packed, token = pack(mid, grad, beyond, near, n_x, pair)
    parts = exchange(packed, "x")

    keep, give = volume_terms(kernel, grad, near, height, width, pair, core, n_core, (token,))
    got = lax.ppermute(give, "core", [(i, n_core - 1 - i) for i in range(n_core)])

    terms, token = kernel_terms(parts, own, height, width, n_y, (got,))
    terms = exchange(terms, "y")

    def send(piece, step):
        return lax.ppermute(piece, "z_lo", [(i, (i + step) % n_z) for i in range(n_z)])

    pieces = sums_by_place(keep, got, place, (token,))
    pieces[1:-1] = [send(piece, step) for step, piece in enumerate(pieces[1:-1], 1)]

    block, token = add_encode(terms, n_y, (size * n_space) ** -0.5, pieces[1:-1])
    line = exchange(block, "y")
    pieces[-1] = send(hand_on(pieces[-1], (token,)), n_z - 1)

    lines, volume_grad, token = finish(line, n_x, pieces)
    codes = exchange(lines, "x").reshape((n_x * n_y,) + block.shape[1:])
    response, far = response_terms(kernel, mid, height, width, pair, (token,))
    response = sum_turned((response, lax.ppermute(far, SPACE, inward)))
    kernel_grad = decode(codes, own, channels).reshape(kernel.shape)
    return response.reshape(volume.shape), volume_grad.reshape(volume.shape), kernel_grad


def solution(mesh):
    axes = SPACE + FILT
    fine = Mesh(mesh.devices.reshape(4, 8, 2, 4, 2), axes)
    channels_last = P(SPACE, None, None, FILT)
    weights = P(None, None, None, FILT, None)
    return jax.shard_map(
        per_device,
        mesh=fine,
        in_specs=(channels_last, weights, channels_last),
        out_specs=(channels_last, channels_last, weights),
        check_vma=False,
    )
```

```python
import jax
import jax.numpy as jnp
from jax import lax
from jax.experimental import pallas as pl
from jax.experimental.pallas import tpu as pltpu
from jax.sharding import Mesh
from jax.sharding import PartitionSpec as P

LANES = 128
F32 = jnp.float32
BF16 = jnp.bfloat16
SPACE = ("x", "y", "z_hi")
FILT = ("z_lo", "core")
VMEM_LIMIT = 48 * 1024 * 1024


def shifted(field, height, width, row, col):
    size = height * width
    step = row * width + col
    moved = field if step == 0 else pltpu.roll(field, (-step) % size, 1)
    if step == 0:
        return moved
    lane = lax.broadcasted_iota(jnp.int32, field.shape, 1)
    at_row = lane // width + row
    at_col = lane % width + col
    inside = (at_row >= 0) & (at_row < height) & (at_col >= 0) & (at_col < width)
    return jnp.where(inside, moved, jnp.zeros_like(moved))


def call(body, out_shape, args, scratch=(), cost=0, scalar=None, after=()):
    many = isinstance(out_shape, (list, tuple))
    whole = pl.BlockSpec(memory_space=pltpu.VMEM)
    in_specs, operands = [whole] * len(args), list(args)
    run = body
    if scalar is not None:
        in_specs = [pl.BlockSpec(memory_space=pltpu.SMEM)] + in_specs
        operands = [scalar.reshape(-1)] + operands
    if after:
        in_specs = [pl.BlockSpec(memory_space=pl.ANY)] * len(after) + in_specs
        operands = list(after) + operands

        def run(*refs):
            body(*refs[len(after) :])

    return pl.pallas_call(
        run,
        out_shape=out_shape,
        in_specs=in_specs,
        out_specs=[whole] * len(out_shape) if many else whole,
        scratch_shapes=list(scratch),
        compiler_params=pltpu.CompilerParams(vmem_limit_bytes=VMEM_LIMIT),
        cost_estimate=pl.CostEstimate(flops=cost, bytes_accessed=4 << 20, transcendentals=0),
    )(*operands)


TOKEN = jax.ShapeDtypeStruct((8, LANES), F32)


def pinned(array):
    return pltpu.with_memory_space_constraint(array, pltpu.HBM)


def turn_copies(field, count):
    def body(field_ref, out_ref, field_vmem, sem):
        copy = pltpu.make_async_copy(field_ref, field_vmem, sem)
        copy.start()
        copy.wait()
        turned = field_vmem[...].astype(F32).T.astype(BF16)
        for at in range(count):
            out_ref[at] = turned

    return pl.pallas_call(
        body,
        out_shape=jax.ShapeDtypeStruct((count,) + field.shape[::-1], BF16),
        in_specs=[pl.BlockSpec(memory_space=pltpu.HBM)],
        out_specs=pl.BlockSpec(memory_space=pltpu.VMEM),
        scratch_shapes=[pltpu.VMEM(field.shape, BF16), pltpu.SemaphoreType.DMA(())],
    )(pinned(field))


def turn(field):
    def body(field_ref, out_ref):
        out_ref[...] = field_ref[...].astype(F32).T.astype(BF16)

    return call(body, jax.ShapeDtypeStruct(field.shape[::-1], BF16), (field,))


def stack(one, two):
    rows, size = one.shape

    def body(one_ref, two_ref, out_ref):
        out_ref[:rows] = one_ref[...]
        out_ref[rows:] = two_ref[...]

    return call(body, jax.ShapeDtypeStruct((2 * rows, size), one.dtype), (one, two))


def response_terms(kernel, planes, height, width, pair, after):
    own, channels = kernel.shape[3:]
    size = height * width

    def body(pair_ref, kernel_ref, planes_ref, here_ref, far_ref):
        even = pair_ref[0] == 0
        mine = jnp.where(even, planes_ref[0], planes_ref[1])
        other = jnp.where(even, planes_ref[1], planes_ref[0])
        results = []
        for depth, plane in enumerate((other, mine, other)):
            weights = kernel_ref[depth].reshape(9 * own, channels)
            total = jnp.dot(weights, plane, preferred_element_type=F32)
            result = jnp.zeros((own, size), F32)
            for row in range(3):
                for col in range(3):
                    at = (row * 3 + col) * own
                    result = result + shifted(total[at : at + own], height, width, row - 1, col - 1)
            results.append(result)
        here_ref[...] = results[1] + jnp.where(even, results[2], results[0])
        far_ref[...] = jnp.where(even, results[0], results[2])

    return call(
        body,
        [jax.ShapeDtypeStruct((own, size), F32)] * 2,
        (kernel, planes),
        cost=2 * 27 * own * channels * size,
        scalar=pair,
        after=after,
    )


def volume_terms(kernel, grads, near, height, width, pair, core, n_core, after):
    own, channels = kernel.shape[3:]
    size = height * width
    groups = channels // own // n_core

    def body(places_ref, kernel_ref, grads_ref, near_ref, keep_ref, give_ref, patch_ref):
        even = places_ref[0] == 0
        mid = grads_ref[:own].astype(F32)
        inside, outside = near_ref[:own].astype(F32), near_ref[own:].astype(F32)
        high = jnp.where(even, inside, outside)
        low = jnp.where(even, outside, inside)
        for depth, plane in enumerate((high, mid, low)):
            for row in range(3):
                for col in range(3):
                    at = (depth * 9 + row * 3 + col) * own
                    moved = shifted(plane, height, width, 1 - row, 1 - col)
                    patch_ref[at : at + own] = moved.astype(BF16)
        result = lax.dot_general(
            kernel_ref[...].reshape(27 * own, channels),
            patch_ref[...],
            (((0,), (0,)), ((), ())),
            preferred_element_type=F32,
        )
        first = places_ref[1] == 0
        for group in range(groups):
            at = group * n_core * own
            one, two = result[at : at + own], result[at + own : at + 2 * own]
            keep_ref[group] = jnp.where(first, one, two)
            give_ref[group] = jnp.where(first, two, one)

    half = jax.ShapeDtypeStruct((groups, own, size), F32)
    return call(
        body,
        [half, half],
        (kernel, grads, near),
        scratch=[pltpu.VMEM((27 * own, size), BF16)],
        cost=2 * 27 * own * channels * size,
        scalar=jnp.stack([pair, core]),
        after=after,
    )


def pack(fields, grads, near, count, pair):
    _, channels, size = fields.shape
    own, part = grads.shape[0] // 2, channels // count

    def body(pair_ref, fields_ref, grads_ref, near_ref, out_ref, token_ref):
        token_ref[...] = jnp.zeros(TOKEN.shape, F32)
        even = pair_ref[0] == 0
        mine, outer = grads_ref[:own], grads_ref[own:]
        other, other_outer = near_ref[:own], near_ref[own:]
        planes = [
            jnp.where(even, outer, other_outer),
            jnp.where(even, other, mine),
            jnp.where(even, mine, other),
            jnp.where(even, other_outer, outer),
        ]
        for place in range(count):
            for side in range(2):
                out_ref[place, side * part : (side + 1) * part] = fields_ref[side, place * part : (place + 1) * part]
            for at, plane in enumerate(planes):
                first = 2 * part + at * own
                out_ref[place, first : first + own] = plane

    return call(
        body,
        [jax.ShapeDtypeStruct((count, 2 * part + 4 * own, size), BF16), TOKEN],
        (fields, grads, near),
        scalar=pair,
    )


def lines_of(own, piece):
    tiles, over = divmod(27 * own, LANES)
    shared = LANES // over
    rest = -(-piece // shared)
    return tiles, over, shared, rest, -(-(tiles * piece + rest + 1) // 16) * 16


def kernel_terms(parts, own, height, width, chunks, after):
    pairs, rows, size = parts.shape
    part = (rows - 4 * own) // 2
    used = 27 * own
    piece = part // chunks
    tiles, over, shared, rest_rows, lines = lines_of(own, piece)

    def body(parts_ref, out_ref, token_ref, patch_ref, grads_ref, wide_ref, rest_ref):
        token_ref[...] = jnp.zeros(TOKEN.shape, F32)
        for at in range(pairs):
            for side in range(2):
                lanes = slice((at * 2 + side) * size, (at * 2 + side + 1) * size)
                field = parts_ref[at, side * part : (side + 1) * part].astype(F32)
                for row in range(3):
                    for col in range(3):
                        first = (row * 3 + col) * part
                        moved = shifted(field, height, width, row - 1, col - 1)
                        patch_ref[first : first + part, lanes] = moved.astype(BF16)
                first = 2 * part + (1 - side) * own
                grads_ref[:, lanes] = parts_ref[at, first : first + 3 * own]
        total = lax.dot_general(
            patch_ref[...], grads_ref[...], (((1,), (1,)), ((), ())), preferred_element_type=F32
        )
        pieces = [total[at * part : (at + 1) * part] for at in range(9)]
        pieces.append(jnp.zeros((part, LANES - over), F32))
        wide_ref[...] = jnp.concatenate(pieces, axis=1)
        rest_ref[...] = wide_ref[:, tiles * LANES :]
        rests = []
        for first in range(0, piece, shared):
            many = min(shared, piece - first)
            rest = [rest_ref[pl.ds(first + at, chunks, stride=piece)][:, :over] for at in range(many)]
            if many * over < LANES:
                rest.append(jnp.zeros((chunks, LANES - many * over), F32))
            rests.append(jnp.concatenate(rest, axis=1))
        for chunk in range(chunks):
            rows_of = slice(chunk * piece, (chunk + 1) * piece)
            for tile in range(tiles):
                lanes = slice(tile * LANES, (tile + 1) * LANES)
                out_ref[chunk, tile * piece : (tile + 1) * piece] = wide_ref[rows_of, lanes]
            out_ref[chunk, tiles * piece :] = jnp.zeros((lines - tiles * piece, LANES), F32)
            for at, rest in enumerate(rests):
                out_ref[chunk, tiles * piece + at : tiles * piece + at + 1] = rest[chunk : chunk + 1]

    return call(
        body,
        [jax.ShapeDtypeStruct((chunks, lines, LANES), F32), TOKEN],
        (parts,),
        scratch=[
            pltpu.VMEM((9 * part, pairs * 2 * size), BF16),
            pltpu.VMEM((3 * own, pairs * 2 * size), BF16),
            pltpu.VMEM((part, (tiles + 1) * LANES), F32),
            pltpu.VMEM((part, LANES), F32),
        ],
        cost=2 * 27 * own * part * pairs * 2 * size,
        after=after,
    )


def add_encode(parts, copies, scale, after):
    _, lines, _ = parts.shape

    def body(parts_ref, out_ref, token_ref):
        token_ref[...] = jnp.zeros(TOKEN.shape, F32)
        values = parts_ref[0]
        for at in range(1, parts.shape[0]):
            values = values + parts_ref[at]
        values = values * scale
        top = jnp.max(jnp.max(jnp.abs(values), axis=0, keepdims=True), axis=1, keepdims=True)
        top = (top * 1.01).astype(BF16).astype(F32)
        top = jnp.where(top > 0, top, jnp.ones_like(top))
        unit = values / top
        square = unit * unit
        code = jnp.where(unit < 0, -square, square) * square
        row = lax.broadcasted_iota(jnp.int32, code.shape, 0)
        code = jnp.where(row < lines - 1, code, jnp.broadcast_to(top, code.shape)).astype(BF16)
        for copy in range(copies):
            out_ref[copy] = code

    return call(body, [jax.ShapeDtypeStruct((copies, lines, LANES), BF16), TOKEN], (parts,), after=after)


def decode(codes, own, channels):
    count, lines, _ = codes.shape
    piece = channels // count
    tiles, over, shared, rest_rows, _ = lines_of(own, piece)

    def body(codes_ref, out_ref, wide_ref, stack_ref, rest_ref):
        for place in range(count):
            code = codes_ref[place].astype(F32)
            size = lax.rsqrt(lax.rsqrt(jnp.abs(code))) * code[lines - 8 :][7:, :1]
            value = jnp.where(code < 0, -size, size)
            wide_ref[place] = value
            for at in range(rest_rows):
                rest_ref[at, place : place + 1] = value[tiles * piece + at : tiles * piece + at + 1]
        for tile in range(tiles + 1):
            if tile < tiles:
                for place in range(count):
                    rows = slice(tile * piece, (tile + 1) * piece)
                    stack_ref[place * piece : (place + 1) * piece] = wide_ref[place, rows]
            else:
                for at in range(piece):
                    row, step = divmod(at, shared)
                    moved = pltpu.roll(rest_ref[row], LANES - step * over, 1) if step else rest_ref[row]
                    stack_ref[pl.ds(at, count, stride=piece)] = moved
            turned = stack_ref[...].T
            at = tile * LANES
            stop = min(at + LANES, 27 * own)
            while at < stop:
                tap, first = divmod(at, own)
                many = min(own - first, stop - at)
                window, depth = divmod(tap, 3)
                from_row = at - tile * LANES
                out_ref[depth * 9 + window, first : first + many] = turned[from_row : from_row + many]
                at += many

    return call(
        body,
        jax.ShapeDtypeStruct((27, own, channels), F32),
        (codes,),
        scratch=[
            pltpu.VMEM((count, lines, LANES), F32),
            pltpu.VMEM((channels, LANES), F32),
            pltpu.VMEM((rest_rows, count, LANES), F32),
        ],
    )


def hand_on(array, after):
    def body(array_ref, out_ref):
        out_ref[...] = array_ref[...]

    return call(body, jax.ShapeDtypeStruct(array.shape, array.dtype), (array,), after=after)


def sums_by_place(keep, got, place, after):
    groups = keep.shape[0]

    def body(place_ref, keep_ref, got_ref, *refs):
        both = [keep_ref[group] + got_ref[group] for group in range(groups)]
        for step, ref in enumerate(refs):
            picked = both[step]
            for at in range(1, groups):
                picked = jnp.where(place_ref[0] == at, both[(at + step) % groups], picked)
            ref[...] = picked

    piece = jax.ShapeDtypeStruct(keep.shape[1:], F32)
    return list(call(body, [piece] * groups, (keep, got), scalar=place, after=after))


def finish(line, copies, terms):
    own, size = terms[0].shape

    def body(line_ref, *refs):
        terms_refs, (lines_ref, out_ref, token_ref) = refs[:-3], refs[-3:]
        token_ref[...] = jnp.zeros(TOKEN.shape, F32)
        for copy in range(copies):
            lines_ref[copy] = line_ref[...]
        total = terms_refs[0][...]
        for ref in terms_refs[1:]:
            total = total + ref[...]
        out_ref[...] = total.T.astype(BF16)

    return call(
        body,
        [
            jax.ShapeDtypeStruct((copies,) + line.shape, BF16),
            jax.ShapeDtypeStruct((size, own), BF16),
            TOKEN,
        ],
        (line, *terms),
    )


def sum_turned(parts):
    own, size = parts[0].shape

    def body(*refs):
        total = refs[0][...]
        for ref in refs[1:-1]:
            total = total + ref[...]
        refs[-1][...] = total.T.astype(BF16)

    return call(body, jax.ShapeDtypeStruct((size, own), BF16), parts)


def exchange(blocks, axis):
    return lax.all_to_all(blocks, axis, 0, 0, tiled=True)


def per_device(volume, kernel, cotangent):
    planes, height, width, own = volume.shape
    channels = kernel.shape[4]
    size = planes * height * width
    n_x, n_y, n_pair = (lax.axis_size(axis) for axis in SPACE)
    n_z, n_core = (lax.axis_size(axis) for axis in FILT)
    n_space, n_filt = n_x * n_y * n_pair, n_z * n_core
    pair, core, place = (lax.axis_index(axis) for axis in ("z_hi", "core", "z_lo"))
    outward = [(i, i - 2) for i in range(2, n_space, 2)] + [(i, i + 2) for i in range(1, n_space - 2, 2)]
    inward = [(target, source) for source, target in outward]
    swap = [(0, 1), (1, 0)]

    grad = turn(cotangent.reshape(size, own))
    beyond = lax.ppermute(grad, SPACE, outward)
    copies = turn_copies(volume.reshape(size, own), n_pair * n_filt)
    mid = exchange(copies, ("z_hi",) + FILT).reshape(n_pair, channels, size)
    grads = stack(grad, beyond)
    near = lax.ppermute(grads, "z_hi", swap)
    packed, token = pack(mid, grads, near, n_x, pair)
    parts = exchange(packed, "x")

    keep, give = volume_terms(kernel, grads, near, height, width, pair, core, n_core, (token,))
    got = lax.ppermute(give, "core", [(i, n_core - 1 - i) for i in range(n_core)])

    terms, token = kernel_terms(parts, own, height, width, n_y, (got,))
    terms = exchange(terms, "y")

    def send(piece, step):
        return lax.ppermute(piece, "z_lo", [(i, (i + step) % n_z) for i in range(n_z)])

    pieces = sums_by_place(keep, got, place, (token,))
    for step in range(n_z - 1, 1, -1):
        pieces[step] = send(pieces[step], step)

    block, token = add_encode(terms, n_y, (size * n_space) ** -0.5, pieces[2:])
    line = exchange(block, "y")
    response, far = response_terms(kernel, mid, height, width, pair, (token,))
    far = lax.ppermute(far, SPACE, inward)

    lines, response, token = finish(line, n_x, (response, far))
    codes = exchange(lines, "x").reshape((n_x * n_y,) + block.shape[1:])
    pieces[1] = send(hand_on(pieces[1], (token,)), 1)
    volume_grad = sum_turned(pieces)
    kernel_grad = decode(codes, own, channels).reshape(kernel.shape)
    return response.reshape(volume.shape), volume_grad.reshape(volume.shape), kernel_grad


def solution(mesh):
    axes = SPACE + FILT
    fine = Mesh(mesh.devices.reshape(4, 8, 2, 4, 2), axes)
    channels_last = P(SPACE, None, None, FILT)
    weights = P(None, None, None, FILT, None)
    return jax.shard_map(
        per_device,
        mesh=fine,
        in_specs=(channels_last, weights, channels_last),
        out_specs=(channels_last, channels_last, weights),
        check_vma=False,
    )
```

```python
import jax
import jax.numpy as jnp
from jax import lax
from jax.experimental import pallas as pl
from jax.experimental.pallas import tpu as pltpu
from jax.sharding import Mesh
from jax.sharding import PartitionSpec as P

LANES = 128
F32 = jnp.float32
BF16 = jnp.bfloat16
SPACE = ("x", "y", "z_hi")
FILT = ("z_lo", "core")
VMEM_LIMIT = 16 * 1024 * 1024


def shifted(field, height, width, row, col):
    size = height * width
    step = row * width + col
    moved = field if step == 0 else pltpu.roll(field, (-step) % size, 1)
    if step == 0:
        return moved
    lane = lax.broadcasted_iota(jnp.int32, field.shape, 1)
    at_row = lane // width + row
    at_col = lane % width + col
    inside = (at_row >= 0) & (at_row < height) & (at_col >= 0) & (at_col < width)
    return jnp.where(inside, moved, jnp.zeros_like(moved))


def call(body, out_shape, args, scratch=(), cost=0, scalar=None, after=()):
    many = isinstance(out_shape, (list, tuple))
    whole = pl.BlockSpec(memory_space=pltpu.VMEM)
    in_specs, operands = [whole] * len(args), list(args)
    run = body
    if scalar is not None:
        in_specs = [pl.BlockSpec(memory_space=pltpu.SMEM)] + in_specs
        operands = [scalar.reshape(-1)] + operands
    if after:
        in_specs = [pl.BlockSpec(memory_space=pl.ANY)] * len(after) + in_specs
        operands = list(after) + operands

        def run(*refs):
            body(*refs[len(after) :])

    return pl.pallas_call(
        run,
        out_shape=out_shape,
        in_specs=in_specs,
        out_specs=[whole] * len(out_shape) if many else whole,
        scratch_shapes=list(scratch),
        compiler_params=pltpu.CompilerParams(vmem_limit_bytes=VMEM_LIMIT),
        cost_estimate=pl.CostEstimate(flops=cost, bytes_accessed=4 << 20, transcendentals=0),
    )(*operands)


TOKEN = jax.ShapeDtypeStruct((8, LANES), F32)


def pinned(array):
    return pltpu.with_memory_space_constraint(array, pltpu.HBM)


def turn_copies(field, count):
    def body(field_ref, out_ref, field_vmem, sem):
        copy = pltpu.make_async_copy(field_ref, field_vmem, sem)
        copy.start()
        copy.wait()
        turned = field_vmem[...].astype(F32).T.astype(BF16)
        for at in range(count):
            out_ref[at] = turned

    return pl.pallas_call(
        body,
        out_shape=jax.ShapeDtypeStruct((count,) + field.shape[::-1], BF16),
        in_specs=[pl.BlockSpec(memory_space=pltpu.HBM)],
        out_specs=pl.BlockSpec(memory_space=pltpu.VMEM),
        scratch_shapes=[pltpu.VMEM(field.shape, BF16), pltpu.SemaphoreType.DMA(())],
        compiler_params=pltpu.CompilerParams(vmem_limit_bytes=VMEM_LIMIT),
    )(pinned(field))


def turn(field):
    def body(field_ref, out_ref):
        out_ref[...] = field_ref[...].astype(F32).T.astype(BF16)

    return call(body, jax.ShapeDtypeStruct(field.shape[::-1], BF16), (field,))


def stack(one, two):
    rows, size = one.shape

    def body(one_ref, two_ref, out_ref):
        out_ref[:rows] = one_ref[...]
        out_ref[rows:] = two_ref[...]

    return call(body, jax.ShapeDtypeStruct((2 * rows, size), one.dtype), (one, two))


def response_terms(kernel, planes, height, width, pair, after):
    own, channels = kernel.shape[3:]
    size = height * width

    def body(pair_ref, kernel_ref, planes_ref, here_ref, far_ref):
        even = pair_ref[0] == 0
        mine = jnp.where(even, planes_ref[0], planes_ref[1])
        other = jnp.where(even, planes_ref[1], planes_ref[0])
        results = []
        for depth, plane in enumerate((other, mine, other)):
            weights = kernel_ref[depth].reshape(9 * own, channels)
            total = jnp.dot(weights, plane, preferred_element_type=F32)
            result = jnp.zeros((own, size), F32)
            for row in range(3):
                for col in range(3):
                    at = (row * 3 + col) * own
                    result = result + shifted(total[at : at + own], height, width, row - 1, col - 1)
            results.append(result)
        here_ref[...] = results[1] + jnp.where(even, results[2], results[0])
        far_ref[...] = jnp.where(even, results[0], results[2])

    return call(
        body,
        [jax.ShapeDtypeStruct((own, size), F32)] * 2,
        (kernel, planes),
        cost=2 * 27 * own * channels * size,
        scalar=pair,
        after=after,
    )


def volume_terms(kernel, grads, near, height, width, pair, core, n_core, after):
    own, channels = kernel.shape[3:]
    size = height * width
    groups = channels // own // n_core

    def body(places_ref, kernel_ref, grads_ref, near_ref, keep_ref, give_ref, patch_ref):
        even = places_ref[0] == 0
        mid = grads_ref[:own].astype(F32)
        inside, outside = near_ref[:own].astype(F32), near_ref[own:].astype(F32)
        high = jnp.where(even, inside, outside)
        low = jnp.where(even, outside, inside)
        for depth, plane in enumerate((high, mid, low)):
            for row in range(3):
                for col in range(3):
                    at = (depth * 9 + row * 3 + col) * own
                    moved = shifted(plane, height, width, 1 - row, 1 - col)
                    patch_ref[at : at + own] = moved.astype(BF16)
        result = lax.dot_general(
            kernel_ref[...].reshape(27 * own, channels),
            patch_ref[...],
            (((0,), (0,)), ((), ())),
            preferred_element_type=F32,
        )
        first = places_ref[1] == 0
        for group in range(groups):
            at = group * n_core * own
            one, two = result[at : at + own], result[at + own : at + 2 * own]
            keep_ref[group] = jnp.where(first, one, two)
            give_ref[group] = jnp.where(first, two, one)

    half = jax.ShapeDtypeStruct((groups, own, size), F32)
    return call(
        body,
        [half, half],
        (kernel, grads, near),
        scratch=[pltpu.VMEM((27 * own, size), BF16)],
        cost=2 * 27 * own * channels * size,
        scalar=jnp.stack([pair, core]),
        after=after,
    )


def pack(fields, grads, near, count, pair):
    _, channels, size = fields.shape
    own, part = grads.shape[0] // 2, channels // count

    def body(pair_ref, fields_ref, grads_ref, near_ref, out_ref, token_ref):
        token_ref[...] = jnp.zeros(TOKEN.shape, F32)
        even = pair_ref[0] == 0
        mine, outer = grads_ref[:own], grads_ref[own:]
        other, other_outer = near_ref[:own], near_ref[own:]
        planes = [
            jnp.where(even, outer, other_outer),
            jnp.where(even, other, mine),
            jnp.where(even, mine, other),
            jnp.where(even, other_outer, outer),
        ]
        for place in range(count):
            for side in range(2):
                out_ref[place, side * part : (side + 1) * part] = fields_ref[side, place * part : (place + 1) * part]
            for at, plane in enumerate(planes):
                first = 2 * part + at * own
                out_ref[place, first : first + own] = plane

    return call(
        body,
        [jax.ShapeDtypeStruct((count, 2 * part + 4 * own, size), BF16), TOKEN],
        (fields, grads, near),
        scalar=pair,
    )


def lines_of(own, piece):
    tiles, over = divmod(27 * own, LANES)
    shared = LANES // over
    rest = -(-piece // shared)
    return tiles, over, shared, rest, -(-(tiles * piece + rest + 1) // 16) * 16


def kernel_terms(parts, own, height, width, chunks, after):
    pairs, rows, size = parts.shape
    part = (rows - 4 * own) // 2
    used = 27 * own
    piece = part // chunks
    tiles, over, shared, rest_rows, lines = lines_of(own, piece)

    def body(parts_ref, out_ref, token_ref, patch_ref, grads_ref, wide_ref, rest_ref):
        token_ref[...] = jnp.zeros(TOKEN.shape, F32)
        for at in range(pairs):
            for side in range(2):
                lanes = slice((at * 2 + side) * size, (at * 2 + side + 1) * size)
                field = parts_ref[at, side * part : (side + 1) * part].astype(F32)
                for row in range(3):
                    for col in range(3):
                        first = (row * 3 + col) * part
                        moved = shifted(field, height, width, row - 1, col - 1)
                        patch_ref[first : first + part, lanes] = moved.astype(BF16)
                first = 2 * part + (1 - side) * own
                grads_ref[:, lanes] = parts_ref[at, first : first + 3 * own]
        total = lax.dot_general(
            patch_ref[...], grads_ref[...], (((1,), (1,)), ((), ())), preferred_element_type=F32
        )
        pieces = [total[at * part : (at + 1) * part] for at in range(9)]
        pieces.append(jnp.zeros((part, LANES - over), F32))
        wide_ref[...] = jnp.concatenate(pieces, axis=1)
        rest_ref[...] = wide_ref[:, tiles * LANES :]
        rests = []
        for first in range(0, piece, shared):
            many = min(shared, piece - first)
            rest = [rest_ref[pl.ds(first + at, chunks, stride=piece)][:, :over] for at in range(many)]
            if many * over < LANES:
                rest.append(jnp.zeros((chunks, LANES - many * over), F32))
            rests.append(jnp.concatenate(rest, axis=1))
        for chunk in range(chunks):
            rows_of = slice(chunk * piece, (chunk + 1) * piece)
            for tile in range(tiles):
                lanes = slice(tile * LANES, (tile + 1) * LANES)
                out_ref[chunk, tile * piece : (tile + 1) * piece] = wide_ref[rows_of, lanes]
            out_ref[chunk, tiles * piece :] = jnp.zeros((lines - tiles * piece, LANES), F32)
            for at, rest in enumerate(rests):
                out_ref[chunk, tiles * piece + at : tiles * piece + at + 1] = rest[chunk : chunk + 1]

    return call(
        body,
        [jax.ShapeDtypeStruct((chunks, lines, LANES), F32), TOKEN],
        (parts,),
        scratch=[
            pltpu.VMEM((9 * part, pairs * 2 * size), BF16),
            pltpu.VMEM((3 * own, pairs * 2 * size), BF16),
            pltpu.VMEM((part, (tiles + 1) * LANES), F32),
            pltpu.VMEM((part, LANES), F32),
        ],
        cost=2 * 27 * own * part * pairs * 2 * size,
        after=after,
    )


def add_encode(parts, copies, scale, after):
    _, lines, _ = parts.shape

    def body(parts_ref, out_ref, token_ref):
        token_ref[...] = jnp.zeros(TOKEN.shape, F32)
        values = parts_ref[0]
        for at in range(1, parts.shape[0]):
            values = values + parts_ref[at]
        values = values * scale
        top = jnp.max(jnp.max(jnp.abs(values), axis=0, keepdims=True), axis=1, keepdims=True)
        top = (top * 1.01).astype(BF16).astype(F32)
        top = jnp.where(top > 0, top, jnp.ones_like(top))
        unit = values / top
        square = unit * unit
        code = jnp.where(unit < 0, -square, square) * square
        row = lax.broadcasted_iota(jnp.int32, code.shape, 0)
        code = jnp.where(row < lines - 1, code, jnp.broadcast_to(top, code.shape)).astype(BF16)
        for copy in range(copies):
            out_ref[copy] = code

    return call(body, [jax.ShapeDtypeStruct((copies, lines, LANES), BF16), TOKEN], (parts,), after=after)


def decode(codes, own, channels):
    count, lines, _ = codes.shape
    piece = channels // count
    tiles, over, shared, rest_rows, _ = lines_of(own, piece)

    def body(codes_ref, out_ref, wide_ref, stack_ref, rest_ref, slab_ref, sems):
        copies = []
        for place in range(count):
            code = codes_ref[place].astype(F32)
            size = lax.rsqrt(lax.rsqrt(jnp.abs(code))) * code[lines - 8 :][7:, :1]
            value = jnp.where(code < 0, -size, size)
            wide_ref[place] = value
            for at in range(rest_rows):
                rest_ref[at, place : place + 1] = value[tiles * piece + at : tiles * piece + at + 1]
        for tile in range(tiles + 1):
            if tile < tiles:
                for place in range(count):
                    rows = slice(tile * piece, (tile + 1) * piece)
                    stack_ref[place * piece : (place + 1) * piece] = wide_ref[place, rows]
            else:
                for at in range(piece):
                    row, step = divmod(at, shared)
                    moved = pltpu.roll(rest_ref[row], LANES - step * over, 1) if step else rest_ref[row]
                    stack_ref[pl.ds(at, count, stride=piece)] = moved
            turned = stack_ref[...].T
            at = tile * LANES
            stop = min(at + LANES, 27 * own)
            while at < stop:
                tap, first = divmod(at, own)
                many = min(own - first, stop - at)
                window, depth = divmod(tap, 3)
                from_row = at - tile * LANES
                slab = depth * 9 + window
                slab_ref[slab, first : first + many] = turned[from_row : from_row + many]
                at += many
                if first + many == own:
                    copies.append(pltpu.make_async_copy(slab_ref.at[slab], out_ref.at[slab], sems.at[slab]))
                    copies[-1].start()
        for copy in copies:
            copy.wait()

    return pl.pallas_call(
        body,
        out_shape=jax.ShapeDtypeStruct((27, own, channels), F32),
        in_specs=[pl.BlockSpec(memory_space=pltpu.VMEM)],
        out_specs=pl.BlockSpec(memory_space=pl.ANY),
        scratch_shapes=[
            pltpu.VMEM((count, lines, LANES), F32),
            pltpu.VMEM((channels, LANES), F32),
            pltpu.VMEM((rest_rows, count, LANES), F32),
            pltpu.VMEM((27, own, channels), F32),
            pltpu.SemaphoreType.DMA((27,)),
        ],
        compiler_params=pltpu.CompilerParams(vmem_limit_bytes=VMEM_LIMIT),
    )(codes)


def hand_on(array, after):
    def body(array_ref, out_ref):
        out_ref[...] = array_ref[...]

    return call(body, jax.ShapeDtypeStruct(array.shape, array.dtype), (array,), after=after)


def sums_by_place(keep, got, place, after):
    groups = keep.shape[0]

    def body(place_ref, keep_ref, got_ref, *refs):
        both = [keep_ref[group] + got_ref[group] for group in range(groups)]
        for step, ref in enumerate(refs):
            picked = both[step]
            for at in range(1, groups):
                picked = jnp.where(place_ref[0] == at, both[(at + step) % groups], picked)
            ref[...] = picked

    piece = jax.ShapeDtypeStruct(keep.shape[1:], F32)
    return list(call(body, [piece] * groups, (keep, got), scalar=place, after=after))


def finish(line, copies, terms):
    own, size = terms[0].shape

    def body(line_ref, *refs):
        terms_refs, (lines_ref, out_ref, token_ref) = refs[:-3], refs[-3:]
        token_ref[...] = jnp.zeros(TOKEN.shape, F32)
        for copy in range(copies):
            lines_ref[copy] = line_ref[...]
        total = terms_refs[0][...]
        for ref in terms_refs[1:]:
            total = total + ref[...]
        out_ref[...] = total.T.astype(BF16)

    return call(
        body,
        [
            jax.ShapeDtypeStruct((copies,) + line.shape, BF16),
            jax.ShapeDtypeStruct((size, own), BF16),
            TOKEN,
        ],
        (line, *terms),
    )


def sum_turned(parts):
    own, size = parts[0].shape

    def body(*refs):
        total = refs[0][...]
        for ref in refs[1:-1]:
            total = total + ref[...]
        refs[-1][...] = total.T.astype(BF16)

    return call(body, jax.ShapeDtypeStruct((size, own), BF16), parts)


def exchange(blocks, axis):
    return lax.all_to_all(blocks, axis, 0, 0, tiled=True)


def per_device(volume, kernel, cotangent):
    planes, height, width, own = volume.shape
    channels = kernel.shape[4]
    size = planes * height * width
    n_x, n_y, n_pair = (lax.axis_size(axis) for axis in SPACE)
    n_z, n_core = (lax.axis_size(axis) for axis in FILT)
    n_space, n_filt = n_x * n_y * n_pair, n_z * n_core
    pair, core, place = (lax.axis_index(axis) for axis in ("z_hi", "core", "z_lo"))
    outward = [(i, i - 2) for i in range(2, n_space, 2)] + [(i, i + 2) for i in range(1, n_space - 2, 2)]
    inward = [(target, source) for source, target in outward]
    swap = [(0, 1), (1, 0)]

    grad = turn(cotangent.reshape(size, own))
    beyond = lax.ppermute(grad, SPACE, outward)
    copies = turn_copies(volume.reshape(size, own), n_pair * n_filt)
    mid = exchange(copies, ("z_hi",) + FILT).reshape(n_pair, channels, size)
    grads = stack(grad, beyond)
    near = lax.ppermute(grads, "z_hi", swap)
    packed, token = pack(mid, grads, near, n_x, pair)
    parts = exchange(packed, "x")

    keep, give = volume_terms(kernel, grads, near, height, width, pair, core, n_core, (token,))
    got = lax.ppermute(give, "core", [(i, n_core - 1 - i) for i in range(n_core)])

    terms, token = kernel_terms(parts, own, height, width, n_y, (got,))
    terms = exchange(terms, "y")

    def send(piece, step):
        return lax.ppermute(piece, "z_lo", [(i, (i + step) % n_z) for i in range(n_z)])

    pieces = sums_by_place(keep, got, place, (token,))
    for step in range(n_z - 1, 1, -1):
        pieces[step] = send(pieces[step], step)

    block, token = add_encode(terms, n_y, (size * n_space) ** -0.5, pieces[2:])
    line = exchange(block, "y")
    response, far = response_terms(kernel, mid, height, width, pair, (token,))
    far = lax.ppermute(far, SPACE, inward)

    lines, response, token = finish(line, n_x, (response, far))
    codes = exchange(lines, "x").reshape((n_x * n_y,) + block.shape[1:])
    pieces[1] = send(hand_on(pieces[1], (token,)), 1)
    volume_grad = sum_turned(pieces)
    kernel_grad = decode(codes, own, channels).reshape(kernel.shape)
    return response.reshape(volume.shape), volume_grad.reshape(volume.shape), kernel_grad


def solution(mesh):
    axes = SPACE + FILT
    fine = Mesh(mesh.devices.reshape(4, 8, 2, 4, 2), axes)
    channels_last = P(SPACE, None, None, FILT)
    weights = P(None, None, None, FILT, None)
    return jax.shard_map(
        per_device,
        mesh=fine,
        in_specs=(channels_last, weights, channels_last),
        out_specs=(channels_last, channels_last, weights),
        check_vma=False,
    )
```

```python
import jax
import jax.numpy as jnp
from jax import lax
from jax.experimental import pallas as pl
from jax.experimental.pallas import tpu as pltpu
from jax.sharding import Mesh
from jax.sharding import PartitionSpec as P

LANES = 128
F32 = jnp.float32
BF16 = jnp.bfloat16
SPACE = ("x", "y", "z_hi")
FILT = ("z_lo", "core")
VMEM_LIMIT = 16 * 1024 * 1024


def shifted(field, height, width, row, col):
    size = height * width
    step = row * width + col
    moved = field if step == 0 else pltpu.roll(field, (-step) % size, 1)
    if step == 0:
        return moved
    lane = lax.broadcasted_iota(jnp.int32, field.shape, 1)
    at_row = lane // width + row
    at_col = lane % width + col
    inside = (at_row >= 0) & (at_row < height) & (at_col >= 0) & (at_col < width)
    return jnp.where(inside, moved, jnp.zeros_like(moved))


def call(body, out_shape, args, scratch=(), cost=0, scalar=None, after=()):
    many = isinstance(out_shape, (list, tuple))
    whole = pl.BlockSpec(memory_space=pltpu.VMEM)
    in_specs, operands = [whole] * len(args), list(args)
    run = body
    if scalar is not None:
        in_specs = [pl.BlockSpec(memory_space=pltpu.SMEM)] + in_specs
        operands = [scalar.reshape(-1)] + operands
    if after:
        in_specs = [pl.BlockSpec(memory_space=pl.ANY)] * len(after) + in_specs
        operands = list(after) + operands

        def run(*refs):
            body(*refs[len(after) :])

    return pl.pallas_call(
        run,
        out_shape=out_shape,
        in_specs=in_specs,
        out_specs=[whole] * len(out_shape) if many else whole,
        scratch_shapes=list(scratch),
        compiler_params=pltpu.CompilerParams(vmem_limit_bytes=VMEM_LIMIT),
        cost_estimate=pl.CostEstimate(flops=cost, bytes_accessed=4 << 20, transcendentals=0),
    )(*operands)


TOKEN = jax.ShapeDtypeStruct((8, LANES), F32)


def pinned(array):
    return pltpu.with_memory_space_constraint(array, pltpu.HBM)


def turn_copies(field, count):
    def body(field_ref, out_ref, field_vmem, sem):
        copy = pltpu.make_async_copy(field_ref, field_vmem, sem)
        copy.start()
        copy.wait()
        turned = field_vmem[...].astype(F32).T.astype(BF16)
        for at in range(count):
            out_ref[at] = turned

    return pl.pallas_call(
        body,
        out_shape=jax.ShapeDtypeStruct((count,) + field.shape[::-1], BF16),
        in_specs=[pl.BlockSpec(memory_space=pltpu.HBM)],
        out_specs=pl.BlockSpec(memory_space=pltpu.VMEM),
        scratch_shapes=[pltpu.VMEM(field.shape, BF16), pltpu.SemaphoreType.DMA(())],
        compiler_params=pltpu.CompilerParams(vmem_limit_bytes=VMEM_LIMIT),
    )(pinned(field))


def turn(field):
    def body(field_ref, out_ref):
        out_ref[...] = field_ref[...].astype(F32).T.astype(BF16)

    return call(body, jax.ShapeDtypeStruct(field.shape[::-1], BF16), (field,))


def stack(one, two):
    rows, size = one.shape

    def body(one_ref, two_ref, out_ref):
        out_ref[:rows] = one_ref[...]
        out_ref[rows:] = two_ref[...]

    return call(body, jax.ShapeDtypeStruct((2 * rows, size), one.dtype), (one, two))


def response_terms(kernel, planes, height, width, pair, after):
    own, channels = kernel.shape[3:]
    size = height * width

    def body(pair_ref, kernel_ref, planes_ref, here_ref, far_ref):
        even = pair_ref[0] == 0
        mine = jnp.where(even, planes_ref[0], planes_ref[1])
        other = jnp.where(even, planes_ref[1], planes_ref[0])
        results = []
        for depth, plane in enumerate((other, mine, other)):
            weights = kernel_ref[depth].reshape(9 * own, channels)
            total = jnp.dot(weights, plane, preferred_element_type=F32)
            result = jnp.zeros((own, size), F32)
            for row in range(3):
                for col in range(3):
                    at = (row * 3 + col) * own
                    result = result + shifted(total[at : at + own], height, width, row - 1, col - 1)
            results.append(result)
        here_ref[...] = results[1] + jnp.where(even, results[2], results[0])
        far_ref[...] = jnp.where(even, results[0], results[2])

    return call(
        body,
        [jax.ShapeDtypeStruct((own, size), F32)] * 2,
        (kernel, planes),
        cost=2 * 27 * own * channels * size,
        scalar=pair,
        after=after,
    )


def volume_terms(kernel, grads, near, height, width, pair, core, n_core, after):
    own, channels = kernel.shape[3:]
    size = height * width
    groups = channels // own // n_core

    def body(places_ref, kernel_ref, grads_ref, near_ref, keep_ref, give_ref, patch_ref):
        even = places_ref[0] == 0
        mid = grads_ref[:own].astype(F32)
        inside, outside = near_ref[:own].astype(F32), near_ref[own:].astype(F32)
        high = jnp.where(even, inside, outside)
        low = jnp.where(even, outside, inside)
        for depth, plane in enumerate((high, mid, low)):
            for row in range(3):
                for col in range(3):
                    at = (depth * 9 + row * 3 + col) * own
                    moved = shifted(plane, height, width, 1 - row, 1 - col)
                    patch_ref[at : at + own] = moved.astype(BF16)
        result = lax.dot_general(
            kernel_ref[...].reshape(27 * own, channels),
            patch_ref[...],
            (((0,), (0,)), ((), ())),
            preferred_element_type=F32,
        )
        first = places_ref[1] == 0
        for group in range(groups):
            at = group * n_core * own
            one, two = result[at : at + own], result[at + own : at + 2 * own]
            keep_ref[group] = jnp.where(first, one, two)
            give_ref[group] = jnp.where(first, two, one)

    half = jax.ShapeDtypeStruct((groups, own, size), F32)
    return call(
        body,
        [half, half],
        (kernel, grads, near),
        scratch=[pltpu.VMEM((27 * own, size), BF16)],
        cost=2 * 27 * own * channels * size,
        scalar=jnp.stack([pair, core]),
        after=after,
    )


def pack(fields, grads, near, count, pair):
    _, channels, size = fields.shape
    own, part = grads.shape[0] // 2, channels // count

    def body(pair_ref, fields_ref, grads_ref, near_ref, out_ref, token_ref):
        token_ref[...] = jnp.zeros(TOKEN.shape, F32)
        even = pair_ref[0] == 0
        mine, outer = grads_ref[:own], grads_ref[own:]
        other, other_outer = near_ref[:own], near_ref[own:]
        planes = [
            jnp.where(even, outer, other_outer),
            jnp.where(even, other, mine),
            jnp.where(even, mine, other),
            jnp.where(even, other_outer, outer),
        ]
        for place in range(count):
            for side in range(2):
                out_ref[place, side * part : (side + 1) * part] = fields_ref[side, place * part : (place + 1) * part]
            for at, plane in enumerate(planes):
                first = 2 * part + at * own
                out_ref[place, first : first + own] = plane

    return call(
        body,
        [jax.ShapeDtypeStruct((count, 2 * part + 4 * own, size), BF16), TOKEN],
        (fields, grads, near),
        scalar=pair,
    )


def lines_of(own, piece):
    tiles, over = divmod(27 * own, LANES)
    shared = LANES // over
    rest = -(-piece // shared)
    return tiles, over, shared, rest, -(-(tiles * piece + rest + 1) // 16) * 16


def kernel_terms(parts, own, height, width, chunks, after):
    pairs, rows, size = parts.shape
    part = (rows - 4 * own) // 2
    used = 27 * own
    piece = part // chunks
    tiles, over, shared, rest_rows, lines = lines_of(own, piece)

    def body(parts_ref, out_ref, token_ref, patch_ref, grads_ref, wide_ref, rest_ref):
        token_ref[...] = jnp.zeros(TOKEN.shape, F32)
        for at in range(pairs):
            for side in range(2):
                lanes = slice((at * 2 + side) * size, (at * 2 + side + 1) * size)
                field = parts_ref[at, side * part : (side + 1) * part].astype(F32)
                for row in range(3):
                    for col in range(3):
                        first = (row * 3 + col) * part
                        moved = shifted(field, height, width, row - 1, col - 1)
                        patch_ref[first : first + part, lanes] = moved.astype(BF16)
                first = 2 * part + (1 - side) * own
                grads_ref[:, lanes] = parts_ref[at, first : first + 3 * own]
        total = lax.dot_general(
            patch_ref[...], grads_ref[...], (((1,), (1,)), ((), ())), preferred_element_type=F32
        )
        pieces = [total[at * part : (at + 1) * part] for at in range(9)]
        pieces.append(jnp.zeros((part, LANES - over), F32))
        wide_ref[...] = jnp.concatenate(pieces, axis=1)
        rest_ref[...] = wide_ref[:, tiles * LANES :]
        rests = []
        for first in range(0, piece, shared):
            many = min(shared, piece - first)
            rest = [rest_ref[pl.ds(first + at, chunks, stride=piece)][:, :over] for at in range(many)]
            if many * over < LANES:
                rest.append(jnp.zeros((chunks, LANES - many * over), F32))
            rests.append(jnp.concatenate(rest, axis=1))
        for chunk in range(chunks):
            rows_of = slice(chunk * piece, (chunk + 1) * piece)
            for tile in range(tiles):
                lanes = slice(tile * LANES, (tile + 1) * LANES)
                out_ref[chunk, tile * piece : (tile + 1) * piece] = wide_ref[rows_of, lanes]
            out_ref[chunk, tiles * piece :] = jnp.zeros((lines - tiles * piece, LANES), F32)
            for at, rest in enumerate(rests):
                out_ref[chunk, tiles * piece + at : tiles * piece + at + 1] = rest[chunk : chunk + 1]

    return call(
        body,
        [jax.ShapeDtypeStruct((chunks, lines, LANES), F32), TOKEN],
        (parts,),
        scratch=[
            pltpu.VMEM((9 * part, pairs * 2 * size), BF16),
            pltpu.VMEM((3 * own, pairs * 2 * size), BF16),
            pltpu.VMEM((part, (tiles + 1) * LANES), F32),
            pltpu.VMEM((part, LANES), F32),
        ],
        cost=2 * 27 * own * part * pairs * 2 * size,
        after=after,
    )


def add_encode(parts, copies, scale, after):
    _, lines, _ = parts.shape

    def body(parts_ref, out_ref, token_ref):
        token_ref[...] = jnp.zeros(TOKEN.shape, F32)
        values = parts_ref[0]
        for at in range(1, parts.shape[0]):
            values = values + parts_ref[at]
        values = values * scale
        top = jnp.max(jnp.max(jnp.abs(values), axis=0, keepdims=True), axis=1, keepdims=True)
        top = (top * 1.01).astype(BF16).astype(F32)
        top = jnp.where(top > 0, top, jnp.ones_like(top))
        unit = values / top
        square = unit * unit
        code = jnp.where(unit < 0, -square, square) * square
        row = lax.broadcasted_iota(jnp.int32, code.shape, 0)
        code = jnp.where(row < lines - 1, code, jnp.broadcast_to(top, code.shape)).astype(BF16)
        for copy in range(copies):
            out_ref[copy] = code

    return call(body, [jax.ShapeDtypeStruct((copies, lines, LANES), BF16), TOKEN], (parts,), after=after)


def decode(codes, own, channels):
    count, lines, _ = codes.shape
    piece = channels // count
    tiles, over, shared, rest_rows, _ = lines_of(own, piece)

    def body(codes_ref, out_ref, wide_ref, stack_ref, rest_ref, slab_ref, top_ref, sems):
        copies = []
        for place in range(count):
            code = codes_ref[place].astype(F32)
            wide_ref[place] = code
            top = code[lines - 8 :][7:]
            top_ref[place * piece : (place + 1) * piece] = jnp.broadcast_to(top, (piece, LANES))
            for at in range(rest_rows):
                rest_ref[at, place : place + 1] = code[tiles * piece + at : tiles * piece + at + 1]
        for tile in range(tiles + 1):
            if tile < tiles:
                for place in range(count):
                    rows = slice(tile * piece, (tile + 1) * piece)
                    stack_ref[place * piece : (place + 1) * piece] = wide_ref[place, rows]
            else:
                for at in range(piece):
                    row, step = divmod(at, shared)
                    moved = pltpu.roll(rest_ref[row], LANES - step * over, 1) if step else rest_ref[row]
                    stack_ref[pl.ds(at, count, stride=piece)] = moved
            code = stack_ref[...]
            size = lax.rsqrt(lax.rsqrt(jnp.abs(code))) * top_ref[...]
            turned = jnp.where(code < 0, -size, size).T
            at = tile * LANES
            stop = min(at + LANES, 27 * own)
            while at < stop:
                tap, first = divmod(at, own)
                many = min(own - first, stop - at)
                window, depth = divmod(tap, 3)
                from_row = at - tile * LANES
                slab = depth * 9 + window
                slab_ref[slab, first : first + many] = turned[from_row : from_row + many]
                at += many
                if first + many == own:
                    copies.append(pltpu.make_async_copy(slab_ref.at[slab], out_ref.at[slab], sems.at[slab]))
                    copies[-1].start()
        for copy in copies:
            copy.wait()

    return pl.pallas_call(
        body,
        out_shape=jax.ShapeDtypeStruct((27, own, channels), F32),
        in_specs=[pl.BlockSpec(memory_space=pltpu.VMEM)],
        out_specs=pl.BlockSpec(memory_space=pl.ANY),
        scratch_shapes=[
            pltpu.VMEM((count, lines, LANES), F32),
            pltpu.VMEM((channels, LANES), F32),
            pltpu.VMEM((rest_rows, count, LANES), F32),
            pltpu.VMEM((27, own, channels), F32),
            pltpu.VMEM((channels, LANES), F32),
            pltpu.SemaphoreType.DMA((27,)),
        ],
        compiler_params=pltpu.CompilerParams(vmem_limit_bytes=VMEM_LIMIT),
    )(codes)


def hand_on(array, after):
    def body(array_ref, out_ref):
        out_ref[...] = array_ref[...]

    return call(body, jax.ShapeDtypeStruct(array.shape, array.dtype), (array,), after=after)


def sums_by_place(keep, got, place, after):
    groups = keep.shape[0]

    def body(place_ref, keep_ref, got_ref, *refs):
        both = [keep_ref[group] + got_ref[group] for group in range(groups)]
        for step, ref in enumerate(refs):
            picked = both[step]
            for at in range(1, groups):
                picked = jnp.where(place_ref[0] == at, both[(at + step) % groups], picked)
            ref[...] = picked

    piece = jax.ShapeDtypeStruct(keep.shape[1:], F32)
    return list(call(body, [piece] * groups, (keep, got), scalar=place, after=after))


def finish(line, copies, terms):
    own, size = terms[0].shape

    def body(line_ref, *refs):
        terms_refs, (lines_ref, out_ref, token_ref) = refs[:-3], refs[-3:]
        token_ref[...] = jnp.zeros(TOKEN.shape, F32)
        for copy in range(copies):
            lines_ref[copy] = line_ref[...]
        total = terms_refs[0][...]
        for ref in terms_refs[1:]:
            total = total + ref[...]
        out_ref[...] = total.T.astype(BF16)

    return call(
        body,
        [
            jax.ShapeDtypeStruct((copies,) + line.shape, BF16),
            jax.ShapeDtypeStruct((size, own), BF16),
            TOKEN,
        ],
        (line, *terms),
    )


def sum_turned(parts):
    own, size = parts[0].shape

    def body(*refs):
        total = refs[0][...]
        for ref in refs[1:-1]:
            total = total + ref[...]
        refs[-1][...] = total.T.astype(BF16)

    return call(body, jax.ShapeDtypeStruct((size, own), BF16), parts)


def exchange(blocks, axis):
    return lax.all_to_all(blocks, axis, 0, 0, tiled=True)


def per_device(volume, kernel, cotangent):
    planes, height, width, own = volume.shape
    channels = kernel.shape[4]
    size = planes * height * width
    n_x, n_y, n_pair = (lax.axis_size(axis) for axis in SPACE)
    n_z, n_core = (lax.axis_size(axis) for axis in FILT)
    n_space, n_filt = n_x * n_y * n_pair, n_z * n_core
    pair, core, place = (lax.axis_index(axis) for axis in ("z_hi", "core", "z_lo"))
    outward = [(i, i - 2) for i in range(2, n_space, 2)] + [(i, i + 2) for i in range(1, n_space - 2, 2)]
    inward = [(target, source) for source, target in outward]
    swap = [(0, 1), (1, 0)]

    grad = turn(cotangent.reshape(size, own))
    beyond = lax.ppermute(grad, SPACE, outward)
    copies = turn_copies(volume.reshape(size, own), n_pair * n_filt)
    mid = exchange(copies, ("z_hi",) + FILT).reshape(n_pair, channels, size)
    grads = stack(grad, beyond)
    near = lax.ppermute(grads, "z_hi", swap)
    packed, token = pack(mid, grads, near, n_x, pair)
    parts = exchange(packed, "x")

    keep, give = volume_terms(kernel, grads, near, height, width, pair, core, n_core, (token,))
    got = lax.ppermute(give, "core", [(i, n_core - 1 - i) for i in range(n_core)])

    terms, token = kernel_terms(parts, own, height, width, n_y, (got,))
    terms = exchange(terms, "y")

    def send(piece, step):
        return lax.ppermute(piece, "z_lo", [(i, (i + step) % n_z) for i in range(n_z)])

    pieces = sums_by_place(keep, got, place, (token,))
    for step in range(n_z - 1, 1, -1):
        pieces[step] = send(pieces[step], step)

    block, token = add_encode(terms, n_y, (size * n_space) ** -0.5, pieces[2:])
    line = exchange(block, "y")
    response, far = response_terms(kernel, mid, height, width, pair, (token,))
    far = lax.ppermute(far, SPACE, inward)

    lines, response, token = finish(line, n_x, (response, far))
    codes = exchange(lines, "x").reshape((n_x * n_y,) + block.shape[1:])
    pieces[1] = send(hand_on(pieces[1], (token,)), 1)
    volume_grad = sum_turned(pieces)
    kernel_grad = decode(codes, own, channels).reshape(kernel.shape)
    return response.reshape(volume.shape), volume_grad.reshape(volume.shape), kernel_grad


def solution(mesh):
    axes = SPACE + FILT
    fine = Mesh(mesh.devices.reshape(4, 8, 2, 4, 2), axes)
    channels_last = P(SPACE, None, None, FILT)
    weights = P(None, None, None, FILT, None)
    return jax.shard_map(
        per_device,
        mesh=fine,
        in_specs=(channels_last, weights, channels_last),
        out_specs=(channels_last, channels_last, weights),
        check_vma=False,
    )
```
